32 devices in a mesh: space: 16 (over z, x, core), scen: 2 (over y).
Axes of the slice: x: 2, y: 2, z: 4, core: 2. Of those that a mesh axis runs over, the one named last changes fastest.
Arguments:
- dwell_map: bfloat16 [4096, 256], P('space', 'scen'), may hold values from 0 to 1
- target_map: bfloat16 [4096, 256], P('space'), may hold values from -6 to 6
- bound_mask: int32 [4096, 256], P('space', 'scen'), may hold values 0 or 1
- offsets: int32 [4, 2], replicated, may hold values from -32 to 32, as said below
- rate_index: int32 [4, 1], replicated, may hold values from 0 to 3
- rate_table: float32 [4], replicated, may hold values from 0.5 to 2
- row_kernels: bfloat16 [4, 63], replicated, may hold values from -0.75 to 0.75
- col_kernels: bfloat16 [4, 63], replicated, may hold values from -0.75 to 0.75
Outputs:
- dwell_next: bfloat16 [4096, 256], P('space', 'scen')
The draws below stay inside these ranges and needn't reach their ends.
Inputs may be any that keep to these rules, and one draw needn't show every extreme that they name: `offsets`: each entry lies between -32 and 32; in each column some scenario has 32 and another -32. `rate_index`: every level is used by some scenario.
All inputs are finite; a program needn't handle non-finite values. No bound on the sum of `bound_mask` on one device may be relied on, other than what follows from the above.
Results may differ from the reference program's by a relative error of at most 0.014.
Values may be sent and summed in bfloat16 or wider, within the bound.
No kernel may reach another device: no remote copies, remote signals or barrier semaphores. Data moves between devices by JAX's collectives and lax.ppermute only.
A program may use at most 64 MiB of HBM per device.

```python
import math
import jax
import jax.numpy as jnp
from jax import lax

S_DEV = 2
KTAPS = 63
REACH = 32
NRATE = 4
SCEN = 4
H = 4096
W = 256
N_SCEN = 2


def draw_offsets(key, part):
    first_key = jax.random.fold_in(key, 11)
    second_key = jax.random.fold_in(key, 12)
    base = jax.random.randint(first_key, (SCEN, 2), -REACH, REACH + 1)
    order = jax.random.permutation(second_key, SCEN)
    base = base.at[order[0], 0].set(REACH)
    base = base.at[order[1], 0].set(-REACH)
    base = base.at[order[2], 1].set(REACH)
    base = base.at[order[3], 1].set(-REACH)
    return base.astype(jnp.int32)


def plant(result, rng, smallest, largest):
    place = [jax.random.randint(jax.random.fold_in(rng, axis), (), 0, length) for axis, length in enumerate(result.shape)]
    longest = result.shape.index(max(result.shape))
    neighbour = place[:longest] + [(place[longest] + 1) % result.shape[longest]] + place[longest + 1:]
    return result.at[tuple(place)].set(smallest).at[tuple(neighbour)].set(largest)


def steps_of(rng, shape, cuts, low, high):
    loudness = 1.0
    for dim, blocks in cuts:
        draws = jax.random.uniform(jax.random.fold_in(jax.random.fold_in(rng, 6), dim), (blocks,), jnp.float32, low / len(cuts), high / len(cuts))
        loudness = loudness * jnp.repeat(jnp.exp(draws), shape[dim] // blocks).reshape((-1,) + (1,) * (len(shape) - 1 - dim))
    return loudness


def different_ones(rng, rows, count, top, lift):
    sequence = jax.random.permutation(jax.random.fold_in(rng, 1), count)
    favour = sequence
    for power in range(3):
        favour = favour * favour // count
    favour = favour * lift // count
    tickets = jax.random.randint(jax.random.fold_in(rng, 2), (rows, count), 0, 4096) + favour
    sure = jax.random.permutation(jax.random.fold_in(rng, 3), rows)[jnp.arange(count) % rows]
    tickets = jnp.where(jnp.arange(rows)[:, None] == sure[None, :], 1 << 14, tickets)
    priority = tickets * count + jnp.arange(count)
    return lax.top_k(priority.astype(jnp.int32), top)[1].astype(jnp.int32)


def bell_draw(key, extent, deviation, most, cuts=(), kind=jnp.bfloat16):
    values = jax.random.normal(key, extent, jnp.float32) * deviation
    if len(cuts) > 0:
        values = steps_of(key, extent, cuts, -0.22, 0.18) * values
    return jnp.clip(values, min=-most, max=most).astype(kind)


def setup_inputs(seed: int = 0) -> dict:
    seeds = jax.random.split(jax.random.key(seed), 9)
    return {
        "dwell_map": jnp.clip(1.0 * jax.random.uniform(seeds[0], (H, W), jnp.float32) ** steps_of(seeds[0], (H, W), ((0, 16), (1, 2)), -0.2, 0.2), 0.0, 1.0).astype(jnp.bfloat16),
        "target_map": bell_draw(seeds[1], (H, W), 1.0, 6.0, ((0, 16),)),
        "bound_mask": plant((jax.random.randint(seeds[2], (H, W), 0, 2) < 1).astype(jnp.int32), jax.random.fold_in(seeds[2], 1), 0, 1),
        "offsets": draw_offsets(jax.random.fold_in(seeds[8], 71), 0),
        "rate_index": different_ones(seeds[4], SCEN, NRATE, 1, 0),
        "rate_table": jnp.clip(jnp.exp(jax.random.uniform(seeds[5], (NRATE,), jnp.float32, math.log(0.5), math.log(2.0))), 0.5, 2.0),
        "row_kernels": bell_draw(seeds[6], (NRATE, KTAPS), KTAPS ** -0.5, 0.75),
        "col_kernels": bell_draw(seeds[7], (NRATE, KTAPS), KTAPS ** -0.5, 0.75),
    }


step_size = 1.0


def band_line(kernel, start_at, row_count, col_count):
    kernel_line = jnp.zeros((col_count + 1,), kernel.dtype)
    kernel_line = lax.dynamic_update_slice(kernel_line, kernel, (start_at,))
    return jnp.tile(kernel_line, row_count)[: row_count * col_count].reshape(row_count, col_count)


def pick_block(length):
    return 128 if length % 128 == 0 else 32


def along_rows(values, kernel, start_at):
    length = values.shape[0]
    col_block = pick_block(length)
    padded = jnp.pad(values, ((col_block, col_block), (0, 0)))
    pieces = [padded[piece * col_block: piece * col_block + length].reshape(length // col_block, col_block, -1) for piece in range(3)]
    stacked = jnp.concatenate(pieces, axis=1)
    matrix = band_line(kernel, start_at + col_block, col_block, 3 * col_block)
    product = jnp.einsum('cy,nym->ncm', matrix, stacked, precision=lax.Precision.HIGHEST)
    return product.reshape(length, -1)


def along_cols(values, kernel, start_at):
    length = values.shape[1]
    row_count = values.shape[0]
    col_block = pick_block(length)
    padded = jnp.pad(values, ((0, 0), (col_block, col_block)))
    pieces = [padded[:, piece * col_block: piece * col_block + length].reshape(row_count, length // col_block, col_block) for piece in range(3)]
    stacked = jnp.concatenate(pieces, axis=2)
    matrix = band_line(kernel, start_at + col_block, col_block, 3 * col_block)
    product = jnp.einsum('rny,cy->rnc', stacked, matrix, precision=lax.Precision.HIGHEST)
    return product.reshape(row_count, length)


def reference(dwell_map, target_map, bound_mask, offsets, rate_index, rate_table, row_kernels, col_kernels):
    radius = (KTAPS - 1) // 2
    dwell_f = dwell_map.astype(jnp.float32)
    target_f = target_map.astype(jnp.float32)

    def scenario(index):
        level = rate_index[index, 0]
        rate_now = rate_table[level]
        row_taps = row_kernels[level].astype(jnp.float32)
        col_taps = col_kernels[level].astype(jnp.float32)
        shift_rows = offsets[index, 0]
        shift_cols = offsets[index, 1]
        forward = along_rows(dwell_f, row_taps, -radius - shift_rows).astype(jnp.bfloat16)
        forward = lax.optimization_barrier(forward).astype(jnp.float32)
        removal = rate_now * along_cols(forward, col_taps, -radius - shift_cols)
        misfit = lax.optimization_barrier((removal - target_f).astype(jnp.bfloat16)).astype(jnp.float32)
        back_cols = along_cols(misfit, col_taps[::-1], -radius + shift_cols).astype(jnp.bfloat16)
        back_cols = lax.optimization_barrier(back_cols).astype(jnp.float32)
        adjoint = along_rows(back_cols, row_taps[::-1], -radius + shift_rows)
        return (rate_now / SCEN) * adjoint

    def group(summed, device):
        group_sum = jnp.zeros(dwell_map.shape, jnp.float32)
        for member in range(S_DEV):
            group_sum = group_sum + scenario(device * S_DEV + member)
        rounded = lax.optimization_barrier(group_sum.astype(jnp.bfloat16)).astype(jnp.float32)
        return summed + rounded, None

    gradient, unused = lax.scan(group, jnp.zeros(dwell_map.shape, jnp.float32), jnp.arange(N_SCEN, dtype=jnp.int32))
    stepped = dwell_f - step_size * gradient
    return jnp.where(bound_mask == 1, jnp.maximum(stepped, 0.0), stepped).astype(jnp.bfloat16)
```

```python
import functools

import jax
import jax.numpy as jnp
from jax import lax
from jax.experimental import pallas as pl
from jax.experimental.pallas import tpu as pltpu
from jax.sharding import PartitionSpec as P

KTAPS = 63
RADIUS = 31
BLOCK = 128
HALF = 64
STEP_SIZE = 1.0
BF16 = jnp.bfloat16
F32 = jnp.float32


def band(taps, start, width):
    line = jnp.concatenate([taps, jnp.zeros((1, width - KTAPS), F32)], axis=1)
    line = pltpu.roll(jnp.broadcast_to(line, (8, width)), start, 1)
    lines = jnp.broadcast_to(line[0:1], (BLOCK, width))
    return pltpu.roll(lines, 0, 1, stride=1, stride_axis=0).astype(BF16)


def bands_kernel(offsets, levels, row_taps, col_taps, fwd_ref, adj_ref, col_ref):
    scen_total, width = col_ref.shape[0], col_ref.shape[1]
    blocks = width // BLOCK
    turn = (
        lax.broadcasted_iota(jnp.int32, (KTAPS, KTAPS), 0)
        + lax.broadcasted_iota(jnp.int32, (KTAPS, KTAPS), 1)
        == KTAPS - 1
    )
    rows = row_taps[...].astype(F32)
    turned = jnp.dot(
        row_taps[...], turn.astype(F32).astype(BF16), preferred_element_type=F32
    )
    cols = col_taps[...].astype(F32)

    def pick(table, level):
        out = table[0:1]
        for r in range(1, table.shape[0]):
            out = jnp.where(level == r, table[r : r + 1], out)
        return out

    for s in range(scen_total):
        level = levels[s, 0]
        shift_row, shift_col = offsets[s, 0], offsets[s, 1]
        fwd_ref[s * BLOCK : (s + 1) * BLOCK, :] = band(
            pick(rows, level), HALF - RADIUS - shift_row, 2 * BLOCK
        )
        adj_ref[s] = band(pick(turned, level), HALF - RADIUS + shift_row, 2 * BLOCK)
        near = band(pick(cols, level), BLOCK - RADIUS - shift_col, 3 * BLOCK)
        for j in range(blocks):
            for y in range(blocks):
                piece = jnp.zeros((BLOCK, BLOCK), BF16)
                if abs(y - j) <= 1:
                    piece = near[:, (y - j + 1) * BLOCK : (y - j + 2) * BLOCK]
                col_ref[s, j * BLOCK : (j + 1) * BLOCK, y * BLOCK : (y + 1) * BLOCK] = piece


def step_kernel(blocks, place, levels, rates, fwd, adj, col, *refs):
    mids, aboves, belows = refs[:blocks], refs[blocks : 2 * blocks], refs[2 * blocks : 3 * blocks]
    target, bound, out, dwell_all, target_all, fwd_all, back_all = refs[3 * blocks :]
    scen_total = adj.shape[0]
    tile = out.shape[0]
    deep = tile + 2 * HALF
    own, first_row, last_row, first_col, last_col = [place[i] for i in range(5)]
    own_lanes = pl.ds(pl.multiple_of(own, BLOCK), BLOCK)
    if blocks == 2:
        spots = [own_lanes, pl.ds(pl.multiple_of(BLOCK - own, BLOCK), BLOCK)]
    else:
        spots = [own_lanes, pl.ds(0, BLOCK), pl.ds(2 * BLOCK, BLOCK)][:blocks]

    target_all[HALF : HALF + tile, :] = target[...]
    for b, lanes in enumerate(spots):
        dwell_all[0:BLOCK, lanes] = aboves[b][0:BLOCK, :]
        dwell_all[BLOCK : BLOCK + tile, lanes] = mids[b][...]
        dwell_all[BLOCK + tile :, lanes] = belows[b][0:BLOCK, :]
        target_all[0:HALF, lanes] = aboves[b][BLOCK:, :]
        target_all[HALF + tile :, lanes] = belows[b][BLOCK:, :]

    for r in range(deep // BLOCK):
        view = dwell_all[r * BLOCK : (r + 2) * BLOCK, :]
        lines = jnp.dot(fwd[...], view, preferred_element_type=F32).astype(BF16)
        for s in range(scen_total):
            fwd_all[s, r * BLOCK : (r + 1) * BLOCK, :] = lines[s * BLOCK : (s + 1) * BLOCK]

    goal = target_all[...].astype(F32)
    for s in range(scen_total):
        rate = rates[levels[s, 0]]
        removal = lax.dot_general(
            fwd_all[s], col[s], (((1,), (1,)), ((), ())), preferred_element_type=F32
        )
        above_rate = jnp.where(first_row == 1, 0.0, rate)
        below_rate = jnp.where(last_row == 1, 0.0, rate)
        removal = jnp.concatenate(
            [
                above_rate * removal[:HALF],
                rate * removal[HALF : deep - HALF],
                below_rate * removal[deep - HALF :],
            ],
            axis=0,
        )
        misfit = (removal - goal).astype(BF16)
        if blocks > 2:
            lane = lax.broadcasted_iota(jnp.int32, misfit.shape, 1)
            inside = (lane >= first_col * BLOCK) & (lane < (blocks - last_col) * BLOCK)
            misfit = jnp.where(inside, misfit, jnp.zeros_like(misfit))
        back = jnp.dot(misfit, col[s, :, own_lanes], preferred_element_type=F32)
        back_all[s] = ((rate / scen_total) * back).astype(BF16)

    for r in range(tile // BLOCK):
        here = slice(r * BLOCK, (r + 1) * BLOCK)
        gradient = jnp.zeros((BLOCK, BLOCK), F32)
        for s in range(scen_total):
            view = back_all[s, r * BLOCK : (r + 2) * BLOCK, :]
            gradient += jnp.dot(adj[s], view, preferred_element_type=F32)
        stepped = mids[0][here, :].astype(F32) - STEP_SIZE * gradient
        out[here, :] = jnp.where(
            bound[here, :] == 1, jnp.maximum(stepped, 0.0), stepped
        ).astype(BF16)


def shards(
    dwell_map, target_map, bound_mask, offsets, rate_index, rate_table, row_kernels, col_kernels
):
    tile = dwell_map.shape[0]
    n_space, n_scen = lax.axis_size("space"), lax.axis_size("scen")
    space, scen = lax.axis_index("space"), lax.axis_index("scen")
    scen_total = offsets.shape[0]
    blocks = min(n_scen, 3)
    width = blocks * BLOCK
    deep = tile + 2 * HALF

    smem = pl.BlockSpec(memory_space=pltpu.SMEM)
    vmem = pl.BlockSpec(memory_space=pltpu.VMEM)

    sides = {1: [], 2: [1]}.get(n_scen, [-1, 1])

    def moved(x, rows, cols):
        pairs = []
        for i in range(n_space):
            for j in range(n_scen):
                a, b = i + rows, j + cols
                if n_scen == 2:
                    b = b % 2
                if 0 <= a < n_space and 0 <= b < n_scen:
                    pairs.append((a * n_scen + b, i * n_scen + j))
        return lax.ppermute(x, ("space", "scen"), pairs)

    own_target = lax.dynamic_slice_in_dim(target_map, scen * BLOCK, BLOCK, 1)
    to_below = jnp.concatenate([dwell_map[tile - BLOCK :], own_target[tile - HALF :]], axis=0)
    to_above = jnp.concatenate([dwell_map[:BLOCK], own_target[:HALF]], axis=0)
    aboves = [moved(to_below, -1, c) for c in [0] + sides]
    belows = [moved(to_above, 1, c) for c in [0] + sides]
    mids = [dwell_map] + [moved(dwell_map, 0, c) for c in sides]

    fwd, adj, col = pl.pallas_call(
        bands_kernel,
        out_shape=(
            jax.ShapeDtypeStruct((scen_total * BLOCK, 2 * BLOCK), BF16),
            jax.ShapeDtypeStruct((scen_total, BLOCK, 2 * BLOCK), BF16),
            jax.ShapeDtypeStruct((scen_total, width, width), BF16),
        ),
        in_specs=[smem, smem, vmem, vmem],
        out_specs=(vmem, vmem, vmem),
        cost_estimate=pl.CostEstimate(flops=10**8, bytes_accessed=10**6, transcendentals=0),
        name="bands",
    )(offsets, rate_index, row_kernels, col_kernels)

    if n_scen <= 2:
        own = scen * BLOCK
        target = target_map
    else:
        own = jnp.int32(BLOCK)
        target = lax.dynamic_slice_in_dim(
            jnp.pad(target_map, ((0, 0), (BLOCK, BLOCK))), scen * BLOCK, width, 1
        )
    place = jnp.stack(
        [
            own,
            (space == 0).astype(jnp.int32),
            (space == n_space - 1).astype(jnp.int32),
            (scen == 0).astype(jnp.int32),
            (scen == n_scen - 1).astype(jnp.int32),
        ]
    ).astype(jnp.int32)

    return pl.pallas_call(
        functools.partial(step_kernel, blocks),
        out_shape=jax.ShapeDtypeStruct(dwell_map.shape, BF16),
        in_specs=[smem] * 3 + [vmem] * (5 + 3 * blocks),
        out_specs=vmem,
        scratch_shapes=[
            pltpu.VMEM((tile + 2 * BLOCK, width), BF16),
            pltpu.VMEM((deep, width), BF16),
            pltpu.VMEM((scen_total, deep, width), BF16),
            pltpu.VMEM((scen_total, deep, BLOCK), BF16),
        ],
        compiler_params=pltpu.CompilerParams(vmem_limit_bytes=48 * 1024 * 1024),
        cost_estimate=pl.CostEstimate(flops=10**9, bytes_accessed=10**6, transcendentals=0),
        name="step",
    )(place, rate_index, rate_table, fwd, adj, col, *mids, *aboves, *belows, target, bound_mask)


def solution(mesh):
    return jax.shard_map(
        shards,
        mesh=mesh,
        in_specs=(
            P("space", "scen"),
            P("space", None),
            P("space", "scen"),
            P(),
            P(),
            P(),
            P(),
            P(),
        ),
        out_specs=P("space", "scen"),
        check_vma=False,
    )
```

```python
import functools

import jax
import jax.numpy as jnp
from jax import lax
from jax.experimental import pallas as pl
from jax.experimental.pallas import tpu as pltpu
from jax.sharding import PartitionSpec as P

KTAPS = 63
RADIUS = 31
BLOCK = 128
HALF = 64
STEP_SIZE = 1.0
BF16 = jnp.bfloat16
F32 = jnp.float32


def band(taps, start, width):
    line = jnp.concatenate([taps, jnp.zeros((1, width - KTAPS), F32)], axis=1)
    line = pltpu.roll(jnp.broadcast_to(line, (8, width)), start, 1)
    lines = jnp.broadcast_to(line[0:1], (BLOCK, width))
    return pltpu.roll(lines, 0, 1, stride=1, stride_axis=0).astype(BF16)


def bands_kernel(offsets, levels, rates, row_taps, col_taps, fwd_ref, adj_ref, col_ref, rate_ref):
    scen_total, width = col_ref.shape[0], col_ref.shape[1]
    blocks = width // BLOCK
    turn = (
        lax.broadcasted_iota(jnp.int32, (KTAPS, KTAPS), 0)
        + lax.broadcasted_iota(jnp.int32, (KTAPS, KTAPS), 1)
        == KTAPS - 1
    )
    rows = row_taps[...].astype(F32)
    turned = jnp.dot(
        row_taps[...], turn.astype(F32).astype(BF16), preferred_element_type=F32
    )
    cols = col_taps[...].astype(F32)

    def pick(table, level):
        out = table[0:1]
        for r in range(1, table.shape[0]):
            out = jnp.where(level == r, table[r : r + 1], out)
        return out

    for s in range(scen_total):
        level = levels[s]
        rate_ref[s] = jnp.full(rate_ref.shape[1:], rates[level], F32)
        shift_row, shift_col = offsets[0, s], offsets[1, s]
        fwd_ref[s * BLOCK : (s + 1) * BLOCK, :] = band(
            pick(rows, level), HALF - RADIUS - shift_row, 2 * BLOCK
        )
        adj_ref[s] = band(pick(turned, level), HALF - RADIUS + shift_row, 2 * BLOCK)
        near = band(pick(cols, level), BLOCK - RADIUS - shift_col, 3 * BLOCK)
        for j in range(blocks):
            for y in range(blocks):
                piece = jnp.zeros((BLOCK, BLOCK), BF16)
                if abs(y - j) <= 1:
                    piece = near[:, (y - j + 1) * BLOCK : (y - j + 2) * BLOCK]
                col_ref[s, j * BLOCK : (j + 1) * BLOCK, y * BLOCK : (y + 1) * BLOCK] = piece


def step_kernel(blocks, rates, fwd, adj, col, *refs):
    mids, outers = refs[:blocks], refs[blocks : 2 * blocks]
    inners, target, bound, out, dwell_all, target_all, fwd_all, back_all = refs[2 * blocks :]
    scen_total = adj.shape[0]
    tile = out.shape[0]
    deep = tile + 2 * HALF
    space, scen = lax.axis_index("space"), lax.axis_index("scen")
    first_row, last_row = space == 0, space == lax.axis_size("space") - 1
    even = lax.rem(space, 2) == 0
    own = scen * BLOCK if blocks == 2 else (blocks - 1) // 2 * BLOCK
    own_lanes = pl.ds(pl.multiple_of(own, BLOCK), BLOCK)
    if blocks == 2:
        spots = [own_lanes, pl.ds(pl.multiple_of(BLOCK - own, BLOCK), BLOCK)]
    else:
        spots = [own_lanes, pl.ds(0, BLOCK), pl.ds(2 * BLOCK, BLOCK)][:blocks]

    def rows(at, count):
        return pl.ds(pl.multiple_of(at, HALF), count)

    inner_dwell = rows(jnp.where(even, BLOCK + tile, 0), BLOCK)
    outer_dwell = rows(jnp.where(even, 0, BLOCK + tile), BLOCK)
    inner_target = rows(jnp.where(even, HALF + tile, 0), HALF)
    outer_target = rows(jnp.where(even, 0, HALF + tile), HALF)
    target_all[HALF : HALF + tile, :] = target[...]
    for b, lanes in enumerate(spots):
        dwell_all[BLOCK : BLOCK + tile, lanes] = mids[b][...]
        low = blocks * BLOCK + b * HALF
        dwell_all[inner_dwell, lanes] = inners[b * BLOCK : (b + 1) * BLOCK, :]
        target_all[inner_target, lanes] = inners[low : low + HALF, :]
        dwell_all[outer_dwell, lanes] = outers[b][:BLOCK, :]
        target_all[outer_target, lanes] = outers[b][BLOCK:, :]

    @pl.when(first_row | last_row)
    def _():
        dwell_all[outer_dwell, :] = jnp.zeros((BLOCK, blocks * BLOCK), BF16)
        target_all[outer_target, :] = jnp.zeros((HALF, blocks * BLOCK), BF16)

    if blocks > 2:
        for edge, lanes in zip((scen == 0, scen == lax.axis_size("scen") - 1), spots[1:]):

            @pl.when(edge)
            def _():
                dwell_all[:, lanes] = jnp.zeros((tile + 2 * BLOCK, BLOCK), BF16)
                target_all[:, lanes] = jnp.zeros((deep, BLOCK), BF16)

    for r in range(deep // BLOCK):
        view = dwell_all[r * BLOCK : (r + 2) * BLOCK, :]
        lines = jnp.dot(fwd[...], view, preferred_element_type=F32).astype(BF16)
        for s in range(scen_total):
            fwd_all[s, r * BLOCK : (r + 1) * BLOCK, :] = lines[s * BLOCK : (s + 1) * BLOCK]

    goal = target_all[...].astype(F32)
    for s in range(scen_total):
        rate = rates[s, 0:1, 0:1]
        removal = lax.dot_general(
            fwd_all[s], col[s], (((1,), (1,)), ((), ())), preferred_element_type=F32
        )
        removal = jnp.concatenate(
            [
                jnp.where(first_row, 0.0, rate) * removal[:HALF],
                rate * removal[HALF : deep - HALF],
                jnp.where(last_row, 0.0, rate) * removal[deep - HALF :],
            ],
            axis=0,
        )
        misfit = (removal - goal).astype(BF16)
        if blocks > 2:
            lane = lax.broadcasted_iota(jnp.int32, misfit.shape, 1)
            low = jnp.where(scen == 0, BLOCK, 0)
            high = jnp.where(scen == lax.axis_size("scen") - 1, 2 * BLOCK, 3 * BLOCK)
            misfit = jnp.where((lane >= low) & (lane < high), misfit, jnp.zeros_like(misfit))
        back = jnp.dot(misfit, col[s, :, own_lanes], preferred_element_type=F32)
        back_all[s] = ((rate / scen_total) * back).astype(BF16)

    for r in range(tile // BLOCK):
        here = slice(r * BLOCK, (r + 1) * BLOCK)
        gradient = jnp.zeros((BLOCK, BLOCK), F32)
        for s in range(scen_total):
            view = back_all[s, r * BLOCK : (r + 2) * BLOCK, :]
            gradient += jnp.dot(adj[s], view, preferred_element_type=F32)
        stepped = mids[0][here, :].astype(F32) - STEP_SIZE * gradient
        out[here, :] = jnp.where(
            bound[here, :] == 1, jnp.maximum(stepped, 0.0), stepped
        ).astype(BF16)


def shards(
    dwell_map, target_map, bound_mask, offsets, rate_index, rate_table, row_kernels, col_kernels
):
    tile = dwell_map.shape[0]
    n_space, n_scen = lax.axis_size("space"), lax.axis_size("scen")
    space, scen = lax.axis_index("space"), lax.axis_index("scen")
    scen_total = offsets.shape[0]
    blocks = min(n_scen, 3)
    width = blocks * BLOCK
    deep = tile + 2 * HALF

    smem = pl.BlockSpec(memory_space=pltpu.SMEM)
    vmem = pl.BlockSpec(memory_space=pltpu.VMEM)

    sides = {1: [], 2: [1]}.get(n_scen, [-1, 1])

    def moved(x, partner):
        pairs = []
        for i in range(n_space):
            for j in range(n_scen):
                a, b = partner(i, j)
                pairs.append((a * n_scen + b % n_scen, i * n_scen + j))
        return lax.ppermute(x, ("space", "scen"), pairs)

    def side(cols):
        return lambda i, j: (i, j + cols)

    def inner(i, j):
        return i ^ 1, j

    def outer(cols):
        def partner(i, j):
            if i in (0, n_space - 1):
                return i, (j ^ 1 if n_scen % 2 == 0 else j)
            return ((i - 1) ^ 1) + 1, j + cols

        return partner

    odd = lax.rem(space, 2)

    def edge(x, low, count):
        return lax.dynamic_slice_in_dim(x, low * (tile - count), count, 0)

    window = [0] + sides
    columns = [lax.rem(scen + n_scen + c, n_scen) * BLOCK for c in window]
    mids = [dwell_map] + [moved(dwell_map, side(c)) for c in sides]
    to_outer = jnp.concatenate(
        [
            edge(dwell_map, odd, BLOCK),
            lax.dynamic_slice(target_map, (odd * (tile - HALF), columns[0]), (HALF, BLOCK)),
        ],
        axis=0,
    )
    outers = [moved(to_outer, outer(c)) for c in window]
    to_inner = jnp.concatenate(
        [edge(m, 1 - odd, BLOCK) for m in mids]
        + [
            lax.dynamic_slice(target_map, ((1 - odd) * (tile - HALF), c), (HALF, BLOCK))
            for c in columns
        ],
        axis=0,
    )
    inners = moved(to_inner, inner)

    levels = rate_index.reshape(scen_total)
    fwd, adj, col, rates = pl.pallas_call(
        bands_kernel,
        out_shape=(
            pltpu.VMEM((scen_total * BLOCK, 2 * BLOCK), BF16),
            pltpu.VMEM((scen_total, BLOCK, 2 * BLOCK), BF16),
            pltpu.VMEM((scen_total, width, width), BF16),
            pltpu.VMEM((scen_total, 8, BLOCK), F32),
        ),
        in_specs=[smem] * 3 + [vmem] * 2,
        out_specs=(vmem,) * 4,
        cost_estimate=pl.CostEstimate(flops=10**8, bytes_accessed=10**6, transcendentals=0),
        name="bands",
    )(offsets.T, levels, rate_table, row_kernels, col_kernels)

    if n_scen <= 2:
        target = target_map
    else:
        target = lax.dynamic_slice_in_dim(
            jnp.pad(target_map, ((0, 0), (BLOCK, BLOCK))), scen * BLOCK, width, 1
        )

    return pl.pallas_call(
        functools.partial(step_kernel, blocks),
        out_shape=jax.ShapeDtypeStruct(dwell_map.shape, BF16),
        in_specs=[vmem] * (7 + 2 * blocks),
        out_specs=vmem,
        scratch_shapes=[
            pltpu.VMEM((tile + 2 * BLOCK, width), BF16),
            pltpu.VMEM((deep, width), BF16),
            pltpu.VMEM((scen_total, deep, width), BF16),
            pltpu.VMEM((scen_total, deep, BLOCK), BF16),
        ],
        compiler_params=pltpu.CompilerParams(vmem_limit_bytes=48 * 1024 * 1024),
        cost_estimate=pl.CostEstimate(flops=10**9, bytes_accessed=10**6, transcendentals=0),
        name="step",
    )(rates, fwd, adj, col, *mids, *outers, inners, target, bound_mask)


def solution(mesh):
    return jax.shard_map(
        shards,
        mesh=mesh,
        in_specs=(
            P("space", "scen"),
            P("space", None),
            P("space", "scen"),
            P(),
            P(),
            P(),
            P(),
            P(),
        ),
        out_specs=P("space", "scen"),
        check_vma=False,
    )
```

```python
import functools

import jax
import jax.numpy as jnp
from jax import lax
from jax.experimental import pallas as pl
from jax.experimental.pallas import tpu as pltpu
from jax.sharding import PartitionSpec as P

KTAPS = 63
RADIUS = 31
BLOCK = 128
HALF = 64
STEP_SIZE = 1.0
BF16 = jnp.bfloat16
F32 = jnp.float32


def band(taps, start, width):
    line = jnp.concatenate([taps, jnp.zeros((1, width - KTAPS), F32)], axis=1)
    line = pltpu.roll(jnp.broadcast_to(line, (8, width)), start, 1)
    lines = jnp.broadcast_to(line[0:1], (BLOCK, width))
    return pltpu.roll(lines, 0, 1, stride=1, stride_axis=0).astype(BF16)


def bands_kernel(offsets, levels, rates, row_taps, col_taps, fwd_ref, adj_ref, col_ref, rate_ref):
    scen_total, width = col_ref.shape[0], col_ref.shape[1]
    blocks = width // BLOCK
    turn = (
        lax.broadcasted_iota(jnp.int32, (KTAPS, KTAPS), 0)
        + lax.broadcasted_iota(jnp.int32, (KTAPS, KTAPS), 1)
        == KTAPS - 1
    )
    rows = row_taps[...].astype(F32)
    turned = jnp.dot(
        row_taps[...], turn.astype(F32).astype(BF16), preferred_element_type=F32
    )
    cols = col_taps[...].astype(F32)

    def pick(table, level):
        out = table[0:1]
        for r in range(1, table.shape[0]):
            out = jnp.where(level == r, table[r : r + 1], out)
        return out

    for s in range(scen_total):
        level = levels[s]
        rate_ref[s] = jnp.full(rate_ref.shape[1:], rates[level], F32)
        shift_row, shift_col = offsets[0, s], offsets[1, s]
        fwd_ref[s * BLOCK : (s + 1) * BLOCK, :] = band(
            pick(rows, level), HALF - RADIUS - shift_row, 2 * BLOCK
        )
        adj_ref[s] = band(pick(turned, level), HALF - RADIUS + shift_row, 2 * BLOCK)
        near = band(pick(cols, level), BLOCK - RADIUS - shift_col, 3 * BLOCK)
        for j in range(blocks):
            for y in range(blocks):
                piece = jnp.zeros((BLOCK, BLOCK), BF16)
                if abs(y - j) <= 1:
                    piece = near[:, (y - j + 1) * BLOCK : (y - j + 2) * BLOCK]
                col_ref[s, j * BLOCK : (j + 1) * BLOCK, y * BLOCK : (y + 1) * BLOCK] = piece


def step_kernel(blocks, rates, fwd, adj, col, *refs):
    mids, outers = refs[:blocks], refs[blocks : 2 * blocks]
    inners = refs[2 * blocks : 3 * blocks]
    target, bound, out, dwell_all, target_all, fwd_all, back_all = refs[3 * blocks :]
    scen_total = adj.shape[0]
    tile = out.shape[0]
    deep = tile + 2 * HALF
    space, scen = lax.axis_index("space"), lax.axis_index("scen")
    first_row, last_row = space == 0, space == lax.axis_size("space") - 1
    even = lax.rem(space, 2) == 0
    own = scen * BLOCK if blocks == 2 else (blocks - 1) // 2 * BLOCK
    own_lanes = pl.ds(pl.multiple_of(own, BLOCK), BLOCK)
    if blocks == 2:
        spots = [own_lanes, pl.ds(pl.multiple_of(BLOCK - own, BLOCK), BLOCK)]
    else:
        spots = [own_lanes, pl.ds(0, BLOCK), pl.ds(2 * BLOCK, BLOCK)][:blocks]

    def rows(at, count):
        return pl.ds(pl.multiple_of(at, HALF), count)

    inner_dwell = rows(jnp.where(even, BLOCK + tile, 0), BLOCK)
    outer_dwell = rows(jnp.where(even, 0, BLOCK + tile), BLOCK)
    inner_target = rows(jnp.where(even, HALF + tile, 0), HALF)
    outer_target = rows(jnp.where(even, 0, HALF + tile), HALF)
    target_all[HALF : HALF + tile, :] = target[...]
    for b, lanes in enumerate(spots):
        dwell_all[BLOCK : BLOCK + tile, lanes] = mids[b][...]
        dwell_all[inner_dwell, lanes] = inners[b][:BLOCK, :]
        target_all[inner_target, lanes] = inners[b][BLOCK:, :]
        dwell_all[outer_dwell, lanes] = outers[b][:BLOCK, :]
        target_all[outer_target, lanes] = outers[b][BLOCK:, :]

    @pl.when(first_row | last_row)
    def _():
        dwell_all[outer_dwell, :] = jnp.zeros((BLOCK, blocks * BLOCK), BF16)
        target_all[outer_target, :] = jnp.zeros((HALF, blocks * BLOCK), BF16)

    if blocks > 2:
        for edge, lanes in zip((scen == 0, scen == lax.axis_size("scen") - 1), spots[1:]):

            @pl.when(edge)
            def _():
                dwell_all[:, lanes] = jnp.zeros((tile + 2 * BLOCK, BLOCK), BF16)
                target_all[:, lanes] = jnp.zeros((deep, BLOCK), BF16)

    for r in range(deep // BLOCK):
        view = dwell_all[r * BLOCK : (r + 2) * BLOCK, :]
        lines = jnp.dot(fwd[...], view, preferred_element_type=F32).astype(BF16)
        for s in range(scen_total):
            fwd_all[s, r * BLOCK : (r + 1) * BLOCK, :] = lines[s * BLOCK : (s + 1) * BLOCK]

    goal = target_all[...].astype(F32)
    for s in range(scen_total):
        rate = rates[s, 0:1, 0:1]
        removal = lax.dot_general(
            fwd_all[s], col[s], (((1,), (1,)), ((), ())), preferred_element_type=F32
        )
        removal = jnp.concatenate(
            [
                jnp.where(first_row, 0.0, rate) * removal[:HALF],
                rate * removal[HALF : deep - HALF],
                jnp.where(last_row, 0.0, rate) * removal[deep - HALF :],
            ],
            axis=0,
        )
        misfit = (removal - goal).astype(BF16)
        if blocks > 2:
            lane = lax.broadcasted_iota(jnp.int32, misfit.shape, 1)
            low = jnp.where(scen == 0, BLOCK, 0)
            high = jnp.where(scen == lax.axis_size("scen") - 1, 2 * BLOCK, 3 * BLOCK)
            misfit = jnp.where((lane >= low) & (lane < high), misfit, jnp.zeros_like(misfit))
        back = jnp.dot(misfit, col[s, :, own_lanes], preferred_element_type=F32)
        back_all[s] = ((rate / scen_total) * back).astype(BF16)

    for r in range(tile // BLOCK):
        here = slice(r * BLOCK, (r + 1) * BLOCK)
        gradient = jnp.zeros((BLOCK, BLOCK), F32)
        for s in range(scen_total):
            view = back_all[s, r * BLOCK : (r + 2) * BLOCK, :]
            gradient += jnp.dot(adj[s], view, preferred_element_type=F32)
        stepped = mids[0][here, :].astype(F32) - STEP_SIZE * gradient
        out[here, :] = jnp.where(
            bound[here, :] == 1, jnp.maximum(stepped, 0.0), stepped
        ).astype(BF16)


def shards(
    dwell_map, target_map, bound_mask, offsets, rate_index, rate_table, row_kernels, col_kernels
):
    tile = dwell_map.shape[0]
    n_space, n_scen = lax.axis_size("space"), lax.axis_size("scen")
    space, scen = lax.axis_index("space"), lax.axis_index("scen")
    scen_total = offsets.shape[0]
    blocks = min(n_scen, 3)
    width = blocks * BLOCK
    deep = tile + 2 * HALF

    smem = pl.BlockSpec(memory_space=pltpu.SMEM)
    vmem = pl.BlockSpec(memory_space=pltpu.VMEM)

    sides = {1: [], 2: [1]}.get(n_scen, [-1, 1])

    def moved(x, partner):
        pairs = []
        for i in range(n_space):
            for j in range(n_scen):
                a, b = partner(i, j)
                pairs.append((a * n_scen + b % n_scen, i * n_scen + j))
        return lax.ppermute(x, ("space", "scen"), pairs)

    def side(cols):
        return lambda i, j: (i, j + cols)

    def inner(cols):
        return lambda i, j: (i ^ 1, j + cols)

    def outer(cols):
        def partner(i, j):
            if i in (0, n_space - 1):
                return i, (j ^ 1 if n_scen % 2 == 0 else j)
            return ((i - 1) ^ 1) + 1, j + cols

        return partner

    odd = lax.rem(space, 2)

    def edge(x, low, count):
        return lax.dynamic_slice_in_dim(x, low * (tile - count), count, 0)

    window = [0] + sides
    columns = [lax.rem(scen + n_scen + c, n_scen) * BLOCK for c in window]
    mids = [dwell_map] + [moved(dwell_map, side(c)) for c in sides]
    to_outer = jnp.concatenate(
        [
            edge(dwell_map, odd, BLOCK),
            lax.dynamic_slice(target_map, (odd * (tile - HALF), columns[0]), (HALF, BLOCK)),
        ],
        axis=0,
    )
    outers = [moved(to_outer, outer(c)) for c in window]
    to_inner = jnp.concatenate(
        [
            edge(dwell_map, 1 - odd, BLOCK),
            lax.dynamic_slice(target_map, ((1 - odd) * (tile - HALF), columns[0]), (HALF, BLOCK)),
        ],
        axis=0,
    )
    inners = [moved(to_inner, inner(c)) for c in window]

    levels = rate_index.reshape(scen_total)
    fwd, adj, col, rates = pl.pallas_call(
        bands_kernel,
        out_shape=(
            pltpu.VMEM((scen_total * BLOCK, 2 * BLOCK), BF16),
            pltpu.VMEM((scen_total, BLOCK, 2 * BLOCK), BF16),
            pltpu.VMEM((scen_total, width, width), BF16),
            pltpu.VMEM((scen_total, 8, BLOCK), F32),
        ),
        in_specs=[smem] * 3 + [vmem] * 2,
        out_specs=(vmem,) * 4,
        cost_estimate=pl.CostEstimate(flops=10**8, bytes_accessed=10**6, transcendentals=0),
        name="bands",
    )(offsets.T, levels, rate_table, row_kernels, col_kernels)

    if n_scen <= 2:
        target = target_map
    else:
        target = lax.dynamic_slice_in_dim(
            jnp.pad(target_map, ((0, 0), (BLOCK, BLOCK))), scen * BLOCK, width, 1
        )

    return pl.pallas_call(
        functools.partial(step_kernel, blocks),
        out_shape=jax.ShapeDtypeStruct(dwell_map.shape, BF16),
        in_specs=[vmem] * (6 + 3 * blocks),
        out_specs=vmem,
        scratch_shapes=[
            pltpu.VMEM((tile + 2 * BLOCK, width), BF16),
            pltpu.VMEM((deep, width), BF16),
            pltpu.VMEM((scen_total, deep, width), BF16),
            pltpu.VMEM((scen_total, deep, BLOCK), BF16),
        ],
        compiler_params=pltpu.CompilerParams(vmem_limit_bytes=48 * 1024 * 1024),
        cost_estimate=pl.CostEstimate(flops=10**9, bytes_accessed=10**6, transcendentals=0),
        name="step",
    )(rates, fwd, adj, col, *mids, *outers, *inners, target, bound_mask)


def solution(mesh):
    return jax.shard_map(
        shards,
        mesh=mesh,
        in_specs=(
            P("space", "scen"),
            P("space", None),
            P("space", "scen"),
            P(),
            P(),
            P(),
            P(),
            P(),
        ),
        out_specs=P("space", "scen"),
        check_vma=False,
    )
```

```python
import functools

import jax
import jax.numpy as jnp
from jax import lax
from jax.experimental import pallas as pl
from jax.experimental.pallas import tpu as pltpu
from jax.sharding import PartitionSpec as P

KTAPS = 63
RADIUS = 31
BLOCK = 128
HALF = 64
STEP_SIZE = 1.0
BF16 = jnp.bfloat16
F32 = jnp.float32


def band(taps, start, width):
    line = jnp.concatenate([taps, jnp.zeros((1, width - KTAPS), F32)], axis=1)
    line = pltpu.roll(jnp.broadcast_to(line, (8, width)), start, 1)
    lines = jnp.broadcast_to(line[0:1], (BLOCK, width))
    return pltpu.roll(lines, 0, 1, stride=1, stride_axis=0).astype(BF16)


def bands_kernel(offsets, levels, rates, row_taps, col_taps, fwd_ref, adj_ref, col_ref, rate_ref):
    scen_total, width = col_ref.shape[0], col_ref.shape[1]
    blocks = width // BLOCK
    turn = (
        lax.broadcasted_iota(jnp.int32, (KTAPS, KTAPS), 0)
        + lax.broadcasted_iota(jnp.int32, (KTAPS, KTAPS), 1)
        == KTAPS - 1
    )
    rows = row_taps[...].astype(F32)
    turned = jnp.dot(
        row_taps[...], turn.astype(F32).astype(BF16), preferred_element_type=F32
    )
    cols = col_taps[...].astype(F32)

    def pick(table, level):
        out = table[0:1]
        for r in range(1, table.shape[0]):
            out = jnp.where(level == r, table[r : r + 1], out)
        return out

    for s in range(scen_total):
        level = levels[s]
        rate_ref[s] = jnp.full(rate_ref.shape[1:], rates[level], F32)
        shift_row, shift_col = offsets[0, s], offsets[1, s]
        fwd_ref[s * BLOCK : (s + 1) * BLOCK, :] = band(
            pick(rows, level), HALF - RADIUS - shift_row, 2 * BLOCK
        )
        adj_ref[s] = band(pick(turned, level), HALF - RADIUS + shift_row, 2 * BLOCK)
        near = band(pick(cols, level), BLOCK - RADIUS - shift_col, 3 * BLOCK)
        for j in range(blocks):
            for y in range(blocks):
                piece = jnp.zeros((BLOCK, BLOCK), BF16)
                if abs(y - j) <= 1:
                    piece = near[:, (y - j + 1) * BLOCK : (y - j + 2) * BLOCK]
                col_ref[s, j * BLOCK : (j + 1) * BLOCK, y * BLOCK : (y + 1) * BLOCK] = piece


def pack_kernel(dwell, target, inner_own, outer_own, outer_side, inner_side, sems):
    tile = dwell.shape[0]
    odd = lax.rem(lax.axis_index("space"), 2)
    own = pl.ds(pl.multiple_of(lax.axis_index("scen") * BLOCK, BLOCK), BLOCK)
    copies = []
    pairs = ((outer_own, odd), (outer_side, odd), (inner_own, 1 - odd), (inner_side, 1 - odd))
    for out, low in pairs:
        dwell_rows = pl.ds(pl.multiple_of(low * (tile - BLOCK), BLOCK), BLOCK)
        target_rows = pl.ds(pl.multiple_of(low * (tile - HALF), HALF), HALF)
        copies.append((dwell.at[dwell_rows, :], out.at[pl.ds(0, BLOCK), :]))
        copies.append((target.at[target_rows, own], out.at[pl.ds(BLOCK, HALF), :]))
    copies = [pltpu.make_async_copy(a, b, sems.at[i]) for i, (a, b) in enumerate(copies)]
    for copy in copies:
        copy.start()
    for copy in copies:
        copy.wait()


def step_kernel(blocks, rates, fwd, adj, col, *refs):
    groups, at = {}, 1
    mids = refs[:1]
    for name, count in (("S", blocks - 1), ("F", blocks - 1), ("P", blocks - 1), ("O", 1), ("E", 1)):
        groups[name] = refs[at : at + count]
        at += count
    mids = mids + groups["S"]
    outers = groups["O"] + groups["P"]
    inners = groups["E"] + groups["F"]
    target, bound, out, dwell_all, target_all, fwd_all, back_all = refs[3 * blocks :]
    scen_total = adj.shape[0]
    tile = out.shape[0]
    deep = tile + 2 * HALF
    space, scen = lax.axis_index("space"), lax.axis_index("scen")
    first_row, last_row = space == 0, space == lax.axis_size("space") - 1
    even = lax.rem(space, 2) == 0
    own = scen * BLOCK if blocks == 2 else (blocks - 1) // 2 * BLOCK
    own_lanes = pl.ds(pl.multiple_of(own, BLOCK), BLOCK)
    if blocks == 2:
        spots = [own_lanes, pl.ds(pl.multiple_of(BLOCK - own, BLOCK), BLOCK)]
    else:
        spots = [own_lanes, pl.ds(0, BLOCK), pl.ds(2 * BLOCK, BLOCK)][:blocks]

    def rows(at, count):
        return pl.ds(pl.multiple_of(at, HALF), count)

    inner_dwell = rows(jnp.where(even, BLOCK + tile, 0), BLOCK)
    outer_dwell = rows(jnp.where(even, 0, BLOCK + tile), BLOCK)
    inner_target = rows(jnp.where(even, HALF + tile, 0), HALF)
    outer_target = rows(jnp.where(even, 0, HALF + tile), HALF)
    target_all[HALF : HALF + tile, :] = target[...]
    for b, lanes in enumerate(spots):
        dwell_all[BLOCK : BLOCK + tile, lanes] = mids[b][...]
        dwell_all[inner_dwell, lanes] = inners[b][:BLOCK, :]
        target_all[inner_target, lanes] = inners[b][BLOCK:, :]
        dwell_all[outer_dwell, lanes] = outers[b][:BLOCK, :]
        target_all[outer_target, lanes] = outers[b][BLOCK:, :]

    @pl.when(first_row | last_row)
    def _():
        dwell_all[outer_dwell, :] = jnp.zeros((BLOCK, blocks * BLOCK), BF16)
        target_all[outer_target, :] = jnp.zeros((HALF, blocks * BLOCK), BF16)

    if blocks > 2:
        for edge, lanes in zip((scen == 0, scen == lax.axis_size("scen") - 1), spots[1:]):

            @pl.when(edge)
            def _():
                dwell_all[:, lanes] = jnp.zeros((tile + 2 * BLOCK, BLOCK), BF16)
                target_all[:, lanes] = jnp.zeros((deep, BLOCK), BF16)

    for r in range(deep // BLOCK):
        view = dwell_all[r * BLOCK : (r + 2) * BLOCK, :]
        lines = jnp.dot(fwd[...], view, preferred_element_type=F32).astype(BF16)
        for s in range(scen_total):
            fwd_all[s, r * BLOCK : (r + 1) * BLOCK, :] = lines[s * BLOCK : (s + 1) * BLOCK]

    goal = target_all[...].astype(F32)
    for s in range(scen_total):
        rate = rates[s, 0:1, 0:1]
        removal = lax.dot_general(
            fwd_all[s], col[s], (((1,), (1,)), ((), ())), preferred_element_type=F32
        )
        removal = jnp.concatenate(
            [
                jnp.where(first_row, 0.0, rate) * removal[:HALF],
                rate * removal[HALF : deep - HALF],
                jnp.where(last_row, 0.0, rate) * removal[deep - HALF :],
            ],
            axis=0,
        )
        misfit = (removal - goal).astype(BF16)
        if blocks > 2:
            lane = lax.broadcasted_iota(jnp.int32, misfit.shape, 1)
            low = jnp.where(scen == 0, BLOCK, 0)
            high = jnp.where(scen == lax.axis_size("scen") - 1, 2 * BLOCK, 3 * BLOCK)
            misfit = jnp.where((lane >= low) & (lane < high), misfit, jnp.zeros_like(misfit))
        back = jnp.dot(misfit, col[s, :, own_lanes], preferred_element_type=F32)
        back_all[s] = ((rate / scen_total) * back).astype(BF16)

    for r in range(tile // BLOCK):
        here = slice(r * BLOCK, (r + 1) * BLOCK)
        gradient = jnp.zeros((BLOCK, BLOCK), F32)
        for s in range(scen_total):
            view = back_all[s, r * BLOCK : (r + 2) * BLOCK, :]
            gradient += jnp.dot(adj[s], view, preferred_element_type=F32)
        stepped = mids[0][here, :].astype(F32) - STEP_SIZE * gradient
        out[here, :] = jnp.where(
            bound[here, :] == 1, jnp.maximum(stepped, 0.0), stepped
        ).astype(BF16)


def shards(
    dwell_map, target_map, bound_mask, offsets, rate_index, rate_table, row_kernels, col_kernels
):
    tile = dwell_map.shape[0]
    n_space, n_scen = lax.axis_size("space"), lax.axis_size("scen")
    space, scen = lax.axis_index("space"), lax.axis_index("scen")
    scen_total = offsets.shape[0]
    blocks = min(n_scen, 3)
    width = blocks * BLOCK
    deep = tile + 2 * HALF

    smem = pl.BlockSpec(memory_space=pltpu.SMEM)
    vmem = pl.BlockSpec(memory_space=pltpu.VMEM)

    sides = {1: [], 2: [1]}.get(n_scen, [-1, 1])

    def moved(x, partner):
        pairs = []
        for i in range(n_space):
            for j in range(n_scen):
                a, b = partner(i, j)
                pairs.append((a * n_scen + b % n_scen, i * n_scen + j))
        return lax.ppermute(x, ("space", "scen"), pairs)

    def side(cols):
        return lambda i, j: (i, j + cols)

    def inner(cols):
        return lambda i, j: (i ^ 1, j + cols)

    def outer(cols):
        def partner(i, j):
            if i in (0, n_space - 1):
                return i, (j ^ 1 if n_scen % 2 == 0 else j)
            return ((i - 1) ^ 1) + 1, j + cols

        return partner


    window = [0] + sides
    hbm = pl.BlockSpec(memory_space=pltpu.HBM)
    inner_own, outer_own, outer_side, inner_side = pl.pallas_call(
        pack_kernel,
        out_shape=(
            pltpu.VMEM((BLOCK + HALF, BLOCK), BF16),
            pltpu.VMEM((BLOCK + HALF, BLOCK), BF16),
            pltpu.VMEM((BLOCK + HALF, BLOCK), BF16),
            pltpu.VMEM((BLOCK + HALF, BLOCK), BF16),
        ),
        in_specs=[hbm] * 2,
        out_specs=(vmem,) * 4,
        scratch_shapes=[pltpu.SemaphoreType.DMA((8,))],
        cost_estimate=pl.CostEstimate(flops=1000, bytes_accessed=10**6, transcendentals=0),
        name="pack",
    )(dwell_map, target_map)
    mids = [dwell_map] + [moved(dwell_map, side(c)) for c in sides]
    outers = [moved(outer_side if c else outer_own, outer(c)) for c in window]
    inners = [moved(inner_side if c else inner_own, inner(c)) for c in window]

    levels = rate_index.reshape(scen_total)
    fwd, adj, col, rates = pl.pallas_call(
        bands_kernel,
        out_shape=(
            pltpu.VMEM((scen_total * BLOCK, 2 * BLOCK), BF16),
            pltpu.VMEM((scen_total, BLOCK, 2 * BLOCK), BF16),
            pltpu.VMEM((scen_total, width, width), BF16),
            pltpu.VMEM((scen_total, 8, BLOCK), F32),
        ),
        in_specs=[smem] * 3 + [vmem] * 2,
        out_specs=(vmem,) * 4,
        cost_estimate=pl.CostEstimate(flops=10**8, bytes_accessed=10**6, transcendentals=0),
        name="bands",
    )(offsets.T, levels, rate_table, row_kernels, col_kernels)

    if n_scen <= 2:
        target = target_map
    else:
        target = lax.dynamic_slice_in_dim(
            jnp.pad(target_map, ((0, 0), (BLOCK, BLOCK))), scen * BLOCK, width, 1
        )

    return pl.pallas_call(
        functools.partial(step_kernel, blocks),
        out_shape=jax.ShapeDtypeStruct(dwell_map.shape, BF16),
        in_specs=[vmem] * (6 + 3 * blocks),
        out_specs=vmem,
        scratch_shapes=[
            pltpu.VMEM((tile + 2 * BLOCK, width), BF16),
            pltpu.VMEM((deep, width), BF16),
            pltpu.VMEM((scen_total, deep, width), BF16),
            pltpu.VMEM((scen_total, deep, BLOCK), BF16),
        ],
        compiler_params=pltpu.CompilerParams(vmem_limit_bytes=48 * 1024 * 1024),
        cost_estimate=pl.CostEstimate(flops=10**9, bytes_accessed=10**6, transcendentals=0),
        name="step",
    )(rates, fwd, adj, col, mids[0], *mids[1:], *inners[1:], *outers[1:], outers[0], inners[0], target, bound_mask)


def solution(mesh):
    return jax.shard_map(
        shards,
        mesh=mesh,
        in_specs=(
            P("space", "scen"),
            P("space", None),
            P("space", "scen"),
            P(),
            P(),
            P(),
            P(),
            P(),
        ),
        out_specs=P("space", "scen"),
        check_vma=False,
    )
```

```python
import functools

import jax
import jax.numpy as jnp
from jax import lax
from jax.experimental import pallas as pl
from jax.experimental.pallas import tpu as pltpu
from jax.sharding import PartitionSpec as P

KTAPS = 63
RADIUS = 31
BLOCK = 128
HALF = 64
STEP_SIZE = 1.0
BF16 = jnp.bfloat16
F32 = jnp.float32
SMEM = pl.BlockSpec(memory_space=pltpu.SMEM)
VMEM = pl.BlockSpec(memory_space=pltpu.VMEM)
HBM = pl.BlockSpec(memory_space=pltpu.HBM)


def dot(a, b, contract_b=0):
    return lax.dot_general(
        a, b, (((1,), (contract_b,)), ((), ())), preferred_element_type=F32
    )


def band(taps, start, width):
    line = jnp.concatenate([taps, jnp.zeros((1, width - KTAPS), F32)], axis=1)
    line = pltpu.roll(jnp.broadcast_to(line, (8, width)), start, 1)
    lines = jnp.broadcast_to(line[0:1], (BLOCK, width))
    return pltpu.roll(lines, 0, 1, stride=1, stride_axis=0).astype(BF16)


def bands_kernel(
    offsets, levels, rates, row_taps, col_taps, dwell, target, bound,
    fwd_ref, adj_ref, col_ref, scale_ref, dwell_out, target_out, bound_out, sems,
):
    moves = ((dwell, dwell_out), (target, target_out), (bound, bound_out))
    copies = [pltpu.make_async_copy(a, b, sems.at[i]) for i, (a, b) in enumerate(moves)]
    for copy in copies:
        copy.start()
    scen_total, width = col_ref.shape[0], col_ref.shape[1]
    blocks = width // BLOCK
    scen = lax.axis_index("scen")
    turn = (
        lax.broadcasted_iota(jnp.int32, (KTAPS, KTAPS), 0)
        + lax.broadcasted_iota(jnp.int32, (KTAPS, KTAPS), 1)
        == KTAPS - 1
    )
    turn = turn.astype(F32).astype(BF16)
    rows = row_taps[...].astype(F32)
    rows_turned, cols_turned = dot(row_taps[...], turn), dot(col_taps[...], turn)

    def pick(table, level):
        out = table[0:1]
        for r in range(1, table.shape[0]):
            out = jnp.where(level == r, table[r : r + 1], out)
        return out

    for s in range(scen_total):
        level = levels[s]
        rate = rates[level]
        lanes = slice(s * BLOCK, (s + 1) * BLOCK)
        scale_ref[0:1, lanes] = jnp.full((1, BLOCK), rate * rate * (1.0 / scen_total), F32)
        scale_ref[1:2, lanes] = jnp.full((1, BLOCK), rate * (-1.0 / scen_total), F32)
        shift_row, shift_col = offsets[0, s], offsets[1, s]
        fwd_ref[s] = band(pick(rows, level), HALF - RADIUS - shift_row, 2 * BLOCK)
        adj_ref[s] = band(pick(rows_turned, level), HALF - RADIUS + shift_row, 2 * BLOCK)
        near = band(pick(cols_turned, level), BLOCK - RADIUS + shift_col, 3 * BLOCK)
        for y in range(blocks):
            for j in range(blocks):
                piece = jnp.zeros((BLOCK, BLOCK), BF16)
                if abs(j - y) <= 1:
                    piece = near[:, (j - y + 1) * BLOCK : (j - y + 2) * BLOCK]
                col_ref[s, y * BLOCK : (y + 1) * BLOCK, j * BLOCK : (j + 1) * BLOCK] = piece
    if blocks > 2:
        for outside, j in ((scen == 0, 0), (scen == lax.axis_size("scen") - 1, 2)):

            @pl.when(outside)
            def _():
                for s in range(scen_total):
                    col_ref[s, :, j * BLOCK : (j + 1) * BLOCK] = jnp.zeros((width, BLOCK), BF16)

    for copy in copies:
        copy.wait()


def lanes_of(blocks):
    if blocks == 2:
        own = lax.axis_index("scen") * BLOCK
        return [
            pl.ds(pl.multiple_of(own, BLOCK), BLOCK),
            pl.ds(pl.multiple_of(BLOCK - own, BLOCK), BLOCK),
        ]
    return [pl.ds((blocks - 1) // 2 * BLOCK, BLOCK), pl.ds(0, BLOCK), pl.ds(2 * BLOCK, BLOCK)][:blocks]


def pack_kernel(blocks, *refs):
    mids, (target, tile_ref, to_outer, to_inner) = refs[:blocks], refs[blocks:]
    tile = target.shape[0]
    scen = lax.axis_index("scen")
    odd = lax.rem(lax.axis_index("space"), 2)
    for b, lane in enumerate(lanes_of(blocks)):
        tile_ref[:, lane] = mids[b][...]
    if blocks > 2:
        for outside, b in ((scen == 0, 0), (scen == lax.axis_size("scen") - 1, 2)):

            @pl.when(outside)
            def _():
                tile_ref[:, b * BLOCK : (b + 1) * BLOCK] = jnp.zeros((tile, BLOCK), BF16)

    for out, low in ((to_outer, odd), (to_inner, 1 - odd)):
        out[:BLOCK, :] = tile_ref[pl.ds(pl.multiple_of(low * (tile - BLOCK), BLOCK), BLOCK), :]
        out[BLOCK:, :] = target[pl.ds(pl.multiple_of(low * (tile - HALF), HALF), HALF), :]


def own_kernel(
    blocks, scale, fwd, adj, col, tile_ref, target, dwell,
    partial_ref, fold_ref, own_ref, edge_ref, target_all, rhs,
):
    scen_total, width = col.shape[0], col.shape[1]
    tile = tile_ref.shape[0]
    space = lax.axis_index("space")
    own_rows = lanes_of(blocks)[0]
    target_all[:HALF, :] = jnp.zeros((HALF, width), BF16)
    target_all[HALF : HALF + tile, :] = target[...]
    target_all[HALF + tile :, :] = jnp.zeros((HALF, width), BF16)
    for s in range(scen_total):
        here = slice(s * BLOCK, (s + 1) * BLOCK)
        mine = col[s, own_rows, :]
        own_ref[here, :] = mine
        fold_ref[:, here] = dot(col[s], mine, 1).astype(BF16)
    from_dwell = (dot(tile_ref[...], fold_ref[...]) * scale[0:1, :]).astype(BF16)
    from_target = (dot(target_all[...], own_ref[...], 1) * scale[1:2, :]).astype(BF16)
    lane = lax.broadcasted_iota(jnp.int32, (BLOCK, 2 * BLOCK), 1)
    cuts = (
        (space == 0) & (lane < HALF),
        (space == lax.axis_size("space") - 1) & (lane >= 2 * BLOCK - HALF),
    )
    for b in range(2):
        lhs = []
        for s in range(scen_total):
            here = slice(s * BLOCK, (s + 1) * BLOCK)
            back = jnp.where(cuts[b], jnp.zeros((BLOCK, 2 * BLOCK), BF16), adj[s])
            upper, lower = dot(back[:, :BLOCK], fwd[s]), dot(back[:, BLOCK:], fwd[s])
            both = [
                upper[:, :BLOCK].astype(BF16),
                (upper[:, BLOCK:] + lower[:, :BLOCK]).astype(BF16),
                lower[:, BLOCK:].astype(BF16),
            ]
            at = 2 * s * BLOCK
            edge_ref[b, :, at : at + BLOCK] = both[2 * b]
            edge_ref[b, :, at + BLOCK : at + 2 * BLOCK] = back[:, b * BLOCK : (b + 1) * BLOCK]
            lhs += [both[1 - b], both[2 - b], back]
            at = 4 * s * BLOCK
            rhs[at : at + tile, :] = from_dwell[:, here]
            rhs[at + tile : at + tile + 2 * BLOCK, :] = from_target[b * BLOCK : (b + 2) * BLOCK, here]
        gradient = dot(jnp.concatenate(lhs, axis=1), rhs[...])
        half = slice(b * BLOCK, (b + 1) * BLOCK)
        partial_ref[half, :] = dwell[half, :].astype(F32) - STEP_SIZE * gradient


def halo_kernel(scale, fold, own, edge, partial, bound, outer, inner, out, dwell_halo, target_halo):
    width = outer.shape[1]
    scen_total = own.shape[0] // BLOCK
    space = lax.axis_index("space")
    odd = lax.rem(space, 2)
    outer_rows = pl.ds(pl.multiple_of(odd * BLOCK, BLOCK), BLOCK)
    inner_rows = pl.ds(pl.multiple_of((1 - odd) * BLOCK, BLOCK), BLOCK)
    outer_goal = pl.ds(pl.multiple_of(odd * (BLOCK + HALF), HALF), HALF)
    inner_goal = pl.ds(pl.multiple_of((1 - odd) * (BLOCK + HALF), HALF), HALF)
    dwell_halo[inner_rows, :] = inner[:BLOCK, :]
    dwell_halo[outer_rows, :] = outer[:BLOCK, :]
    target_halo[HALF : HALF + BLOCK, :] = jnp.zeros((BLOCK, width), BF16)
    target_halo[inner_goal, :] = inner[BLOCK:, :]
    target_halo[outer_goal, :] = outer[BLOCK:, :]

    @pl.when((space == 0) | (space == lax.axis_size("space") - 1))
    def _():
        dwell_halo[outer_rows, :] = jnp.zeros((BLOCK, width), BF16)
        target_halo[outer_goal, :] = jnp.zeros((HALF, width), BF16)

    from_dwell = (dot(dwell_halo[...], fold[...]) * scale[0:1, :]).astype(BF16)
    from_target = (dot(target_halo[...], own[...], 1) * scale[1:2, :]).astype(BF16)
    for b in range(2):
        half = slice(b * BLOCK, (b + 1) * BLOCK)
        rhs = []
        for s in range(scen_total):
            here = slice(s * BLOCK, (s + 1) * BLOCK)
            rhs += [from_dwell[half, here], from_target[half, here]]
        gradient = dot(edge[b], jnp.concatenate(rhs, axis=0))
        stepped = partial[half, :] - STEP_SIZE * gradient
        out[half, :] = jnp.where(
            bound[half, :] == 1, jnp.maximum(stepped, 0.0), stepped
        ).astype(BF16)


def shards(
    dwell_map, target_map, bound_mask, offsets, rate_index, rate_table, row_kernels, col_kernels
):
    tile = dwell_map.shape[0]
    n_space, n_scen = lax.axis_size("space"), lax.axis_size("scen")
    scen = lax.axis_index("scen")
    scen_total = offsets.shape[0]
    blocks = min(n_scen, 3)
    width = blocks * BLOCK
    sides = {1: [], 2: [1]}.get(n_scen, [-1, 1])

    def moved(x, partner):
        pairs = []
        for i in range(n_space):
            for j in range(n_scen):
                a, b = partner(i, j)
                pairs.append((a * n_scen + b % n_scen, i * n_scen + j))
        return lax.ppermute(x, ("space", "scen"), pairs)

    def side(cols):
        return lambda i, j: (i, j + cols)

    def inner(i, j):
        return i ^ 1, j

    def outer(i, j):
        if i in (0, n_space - 1):
            return i, (j ^ 1 if n_scen % 2 == 0 else j)
        return ((i - 1) ^ 1) + 1, j

    def call(kernel, name, outs, scratch, flops, specs, *args, limit=32 * 1024 * 1024):
        return pl.pallas_call(
            kernel,
            out_shape=outs,
            in_specs=specs,
            out_specs=jax.tree.map(lambda _: VMEM, outs),
            scratch_shapes=scratch,
            compiler_params=pltpu.CompilerParams(vmem_limit_bytes=limit),
            cost_estimate=pl.CostEstimate(
                flops=flops, bytes_accessed=flops // 100, transcendentals=0
            ),
            name=name,
        )(*args)

    if n_scen <= 2:
        target = target_map
    else:
        target = lax.dynamic_slice_in_dim(
            jnp.pad(target_map, ((0, 0), (BLOCK, BLOCK))), scen * BLOCK, width, 1
        )
    neighbours = [moved(dwell_map, side(c)) for c in sides]

    fwd, adj, col, scale, dwell_here, target_here, bound_here = call(
        bands_kernel,
        "bands",
        (
            pltpu.VMEM((scen_total, BLOCK, 2 * BLOCK), BF16),
            pltpu.VMEM((scen_total, BLOCK, 2 * BLOCK), BF16),
            pltpu.VMEM((scen_total, width, width), BF16),
            pltpu.VMEM((8, scen_total * BLOCK), F32),
            pltpu.VMEM(dwell_map.shape, BF16),
            pltpu.VMEM(target.shape, BF16),
            pltpu.VMEM(bound_mask.shape, jnp.int32),
        ),
        [pltpu.SemaphoreType.DMA((3,))],
        10**8,
        [SMEM] * 3 + [VMEM] * 2 + [HBM] * 3,
        offsets.T,
        rate_index.reshape(scen_total),
        rate_table,
        row_kernels,
        col_kernels,
        dwell_map,
        target,
        bound_mask,
        limit=None,
    )
    tile_here, to_outer, to_inner = call(
        functools.partial(pack_kernel, blocks),
        "pack",
        (
            pltpu.VMEM((tile, width), BF16),
            pltpu.VMEM((BLOCK + HALF, width), BF16),
            pltpu.VMEM((BLOCK + HALF, width), BF16),
        ),
        [],
        10**5,
        [VMEM] * (blocks + 1),
        dwell_here,
        *neighbours,
        target_here,
    )
    outer_rows = moved(to_outer, outer)
    inner_rows = moved(to_inner, inner)
    partial, fold, own, edge = call(
        functools.partial(own_kernel, blocks),
        "own",
        (
            pltpu.VMEM((tile, BLOCK), F32),
            pltpu.VMEM((width, scen_total * BLOCK), BF16),
            pltpu.VMEM((scen_total * BLOCK, width), BF16),
            pltpu.VMEM((2, BLOCK, scen_total * 2 * BLOCK), BF16),
        ),
        [
            pltpu.VMEM((tile + 2 * HALF, width), BF16),
            pltpu.VMEM((scen_total * (tile + 2 * BLOCK), BLOCK), BF16),
        ],
        10**9,
        [VMEM] * 7,
        scale,
        fwd,
        adj,
        col,
        tile_here,
        target_here,
        dwell_here,
    )
    return call(
        halo_kernel,
        "halo",
        jax.ShapeDtypeStruct(dwell_map.shape, BF16),
        [pltpu.VMEM((2 * BLOCK, width), BF16), pltpu.VMEM((2 * BLOCK, width), BF16)],
        10**8,
        [VMEM] * 8,
        scale,
        fold,
        own,
        edge,
        partial,
        bound_here,
        outer_rows,
        inner_rows,
    )


def solution(mesh):
    return jax.shard_map(
        shards,
        mesh=mesh,
        in_specs=(
            P("space", "scen"),
            P("space", None),
            P("space", "scen"),
            P(),
            P(),
            P(),
            P(),
            P(),
        ),
        out_specs=P("space", "scen"),
        check_vma=False,
    )
```

```python
import functools

import jax
import jax.numpy as jnp
from jax import lax
from jax.experimental import pallas as pl
from jax.experimental.pallas import tpu as pltpu
from jax.sharding import PartitionSpec as P

KTAPS = 63
RADIUS = 31
BLOCK = 128
HALF = 64
STEP_SIZE = 1.0
BF16 = jnp.bfloat16
F32 = jnp.float32
SMEM = pl.BlockSpec(memory_space=pltpu.SMEM)
VMEM = pl.BlockSpec(memory_space=pltpu.VMEM)
HBM = pl.BlockSpec(memory_space=pltpu.HBM)


def dot(a, b, contract_b=0):
    return lax.dot_general(
        a, b, (((1,), (contract_b,)), ((), ())), preferred_element_type=F32
    )


def band(taps, start, width):
    line = jnp.concatenate([taps, jnp.zeros((1, width - KTAPS), F32)], axis=1)
    line = pltpu.roll(jnp.broadcast_to(line, (8, width)), start, 1)
    lines = jnp.broadcast_to(line[0:1], (BLOCK, width))
    return pltpu.roll(lines, 0, 1, stride=1, stride_axis=0).astype(BF16)


def bands_kernel(
    offsets, levels, rates, row_taps, col_taps, dwell, target, bound,
    fwd_ref, adj_ref, fold_ref, own_ref, edge_ref, ends_ref, scale_ref, dwell_out, target_out, bound_out,
    col_ref, target_ends, sems,
):
    moves = ((target, target_out), (dwell, dwell_out), (bound, bound_out))
    copies = [pltpu.make_async_copy(a, b, sems.at[i]) for i, (a, b) in enumerate(moves)]
    for copy in copies:
        copy.start()
    scen_total, width = col_ref.shape[0], col_ref.shape[1]
    blocks = width // BLOCK
    scen = lax.axis_index("scen")
    own_rows = lanes_of(blocks)[0]
    turn = (
        lax.broadcasted_iota(jnp.int32, (KTAPS, KTAPS), 0)
        + lax.broadcasted_iota(jnp.int32, (KTAPS, KTAPS), 1)
        == KTAPS - 1
    )
    turn = turn.astype(F32).astype(BF16)
    rows = row_taps[...].astype(F32)
    rows_turned, cols_turned = dot(row_taps[...], turn), dot(col_taps[...], turn)

    def pick(table, level):
        out = table[0:1]
        for r in range(1, table.shape[0]):
            out = jnp.where(level == r, table[r : r + 1], out)
        return out

    for s in range(scen_total):
        level = levels[s]
        rate = rates[level]
        here = slice(s * BLOCK, (s + 1) * BLOCK)
        scale_ref[0:1, here] = jnp.full((1, BLOCK), rate * rate * (1.0 / scen_total), F32)
        scale_ref[1:2, here] = jnp.full((1, BLOCK), rate * (-1.0 / scen_total), F32)
        shift_row, shift_col = offsets[0, s], offsets[1, s]
        fwd = band(pick(rows, level), HALF - RADIUS - shift_row, 2 * BLOCK)
        adj = band(pick(rows_turned, level), HALF - RADIUS + shift_row, 2 * BLOCK)
        fwd_ref[s] = fwd
        adj_ref[s] = adj
        upper, lower = adj[:, :BLOCK], adj[:, BLOCK:]
        at = 2 * s * BLOCK
        edge_ref[0, :, at : at + BLOCK] = dot(upper, fwd[:, :BLOCK]).astype(BF16)
        edge_ref[0, :, at + BLOCK : at + 2 * BLOCK] = upper
        edge_ref[1, :, at : at + BLOCK] = dot(lower, fwd[:, BLOCK:]).astype(BF16)
        edge_ref[1, :, at + BLOCK : at + 2 * BLOCK] = lower
        near = band(pick(cols_turned, level), BLOCK - RADIUS + shift_col, 3 * BLOCK)
        for y in range(blocks):
            for j in range(blocks):
                piece = jnp.zeros((BLOCK, BLOCK), BF16)
                if abs(j - y) <= 1:
                    piece = near[:, (j - y + 1) * BLOCK : (j - y + 2) * BLOCK]
                col_ref[s, y * BLOCK : (y + 1) * BLOCK, j * BLOCK : (j + 1) * BLOCK] = piece
    if blocks > 2:
        for outside, j in ((scen == 0, 0), (scen == lax.axis_size("scen") - 1, 2)):

            @pl.when(outside)
            def _():
                for s in range(scen_total):
                    col_ref[s, :, j * BLOCK : (j + 1) * BLOCK] = jnp.zeros((width, BLOCK), BF16)

    for s in range(scen_total):
        here = slice(s * BLOCK, (s + 1) * BLOCK)
        mine = col_ref[s, own_rows, :]
        own_ref[here, :] = mine
        fold_ref[:, here] = dot(col_ref[s], mine, 1).astype(BF16)
    copies[0].wait()
    tile = target.shape[0]
    target_ends[:HALF, :] = target_out[tile - HALF :, :]
    target_ends[HALF : HALF + BLOCK, :] = jnp.zeros((BLOCK, width), BF16)
    target_ends[HALF + BLOCK :, :] = target_out[:HALF, :]
    ends_ref[...] = (dot(target_ends[...], own_ref[...], 1) * scale_ref[1:2, :]).astype(BF16)
    for copy in copies[1:]:
        copy.wait()


def lanes_of(blocks):
    if blocks == 2:
        own = lax.axis_index("scen") * BLOCK
        return [
            pl.ds(pl.multiple_of(own, BLOCK), BLOCK),
            pl.ds(pl.multiple_of(BLOCK - own, BLOCK), BLOCK),
        ]
    return [pl.ds((blocks - 1) // 2 * BLOCK, BLOCK), pl.ds(0, BLOCK), pl.ds(2 * BLOCK, BLOCK)][:blocks]


def send_kernel(blocks, scale, fold, edge, ends, *refs):
    mids, (from_ref, to_outer, to_inner, tile_ref) = refs[:blocks], refs[blocks:]
    scen_total = fold.shape[1] // BLOCK
    tile = tile_ref.shape[0]
    scen = lax.axis_index("scen")
    odd = lax.rem(lax.axis_index("space"), 2)
    for b, lane in enumerate(lanes_of(blocks)):
        tile_ref[:, lane] = mids[b][...]
    if blocks > 2:
        for outside, b in ((scen == 0, 0), (scen == lax.axis_size("scen") - 1, 2)):

            @pl.when(outside)
            def _():
                tile_ref[:, b * BLOCK : (b + 1) * BLOCK] = jnp.zeros((tile, BLOCK), BF16)

    from_dwell = (dot(tile_ref[...], fold[...]) * scale[0:1, :]).astype(BF16)
    from_ref[...] = from_dwell
    terms = []
    for b, rows in enumerate((slice(tile - BLOCK, tile), slice(0, BLOCK))):
        rhs = []
        for s in range(scen_total):
            here = slice(s * BLOCK, (s + 1) * BLOCK)
            rhs += [from_dwell[rows, here], ends[b * BLOCK : (b + 1) * BLOCK, here]]
        terms.append(dot(edge[b], jnp.concatenate(rhs, axis=0)).astype(BF16))
    to_outer[...] = jnp.where(odd == 1, terms[0], terms[1])
    to_inner[...] = jnp.where(odd == 1, terms[1], terms[0])


def own_kernel(scale, fwd, adj, own, from_dwell, target, dwell, partial_ref, target_all, rhs):
    scen_total, width = fwd.shape[0], own.shape[1]
    tile = target.shape[0]
    space = lax.axis_index("space")
    target_all[:HALF, :] = jnp.zeros((HALF, width), BF16)
    target_all[HALF : HALF + tile, :] = target[...]
    target_all[HALF + tile :, :] = jnp.zeros((HALF, width), BF16)
    from_target = (dot(target_all[...], own[...], 1) * scale[1:2, :]).astype(BF16)
    lane = lax.broadcasted_iota(jnp.int32, (BLOCK, 2 * BLOCK), 1)
    cuts = (
        (space == 0) & (lane < HALF),
        (space == lax.axis_size("space") - 1) & (lane >= 2 * BLOCK - HALF),
    )
    for b in range(2):
        lhs = []
        for s in range(scen_total):
            here = slice(s * BLOCK, (s + 1) * BLOCK)
            back = jnp.where(cuts[b], jnp.zeros((BLOCK, 2 * BLOCK), BF16), adj[s])
            upper, lower = dot(back[:, :BLOCK], fwd[s]), dot(back[:, BLOCK:], fwd[s])
            middle = (upper[:, BLOCK:] + lower[:, :BLOCK]).astype(BF16)
            if b == 0:
                lhs += [middle, lower[:, BLOCK:].astype(BF16), back]
            else:
                lhs += [upper[:, :BLOCK].astype(BF16), middle, back]
            at = 4 * s * BLOCK
            rhs[at : at + tile, :] = from_dwell[:, here]
            rhs[at + tile : at + tile + 2 * BLOCK, :] = from_target[b * BLOCK : (b + 2) * BLOCK, here]
        gradient = dot(jnp.concatenate(lhs, axis=1), rhs[...])
        half = slice(b * BLOCK, (b + 1) * BLOCK)
        partial_ref[half, :] = dwell[half, :].astype(F32) - STEP_SIZE * gradient


def finish_kernel(partial, bound, outer, inner, out):
    space = lax.axis_index("space")
    odd = lax.rem(space, 2)
    end = (space == 0) | (space == lax.axis_size("space") - 1)
    tile = out.shape[0]
    for at, terms in ((odd, outer), (1 - odd, inner)):
        half = pl.ds(pl.multiple_of(at * (tile - BLOCK), BLOCK), BLOCK)
        gradient = terms[...].astype(F32)
        if terms is outer:
            gradient = jnp.where(end, jnp.zeros_like(gradient), gradient)
        stepped = partial[half, :] - STEP_SIZE * gradient
        out[half, :] = jnp.where(
            bound[half, :] == 1, jnp.maximum(stepped, 0.0), stepped
        ).astype(BF16)


def shards(
    dwell_map, target_map, bound_mask, offsets, rate_index, rate_table, row_kernels, col_kernels
):
    tile = dwell_map.shape[0]
    n_space, n_scen = lax.axis_size("space"), lax.axis_size("scen")
    scen = lax.axis_index("scen")
    scen_total = offsets.shape[0]
    blocks = min(n_scen, 3)
    width = blocks * BLOCK
    sides = {1: [], 2: [1]}.get(n_scen, [-1, 1])

    def moved(x, partner):
        pairs = []
        for i in range(n_space):
            for j in range(n_scen):
                a, b = partner(i, j)
                pairs.append((a * n_scen + b % n_scen, i * n_scen + j))
        return lax.ppermute(x, ("space", "scen"), pairs)

    def side(cols):
        return lambda i, j: (i, j + cols)

    def inner(i, j):
        return i ^ 1, j

    def outer(i, j):
        if i in (0, n_space - 1):
            return i, (j ^ 1 if n_scen % 2 == 0 else j)
        return ((i - 1) ^ 1) + 1, j

    def call(kernel, name, outs, scratch, flops, specs, *args, limit=32 * 1024 * 1024):
        return pl.pallas_call(
            kernel,
            out_shape=outs,
            in_specs=specs,
            out_specs=jax.tree.map(lambda _: VMEM, outs),
            scratch_shapes=scratch,
            compiler_params=pltpu.CompilerParams(vmem_limit_bytes=limit),
            cost_estimate=pl.CostEstimate(
                flops=flops, bytes_accessed=flops // 100, transcendentals=0
            ),
            name=name,
        )(*args)

    if n_scen <= 2:
        target = target_map
    else:
        target = lax.dynamic_slice_in_dim(
            jnp.pad(target_map, ((0, 0), (BLOCK, BLOCK))), scen * BLOCK, width, 1
        )
    neighbours = [moved(dwell_map, side(c)) for c in sides]

    wide = scen_total * BLOCK
    (fwd, adj, fold, own, edge, ends, scale, dwell_here, target_here, bound_here) = call(
        bands_kernel,
        "bands",
        (
            pltpu.VMEM((scen_total, BLOCK, 2 * BLOCK), BF16),
            pltpu.VMEM((scen_total, BLOCK, 2 * BLOCK), BF16),
            pltpu.VMEM((width, wide), BF16),
            pltpu.VMEM((wide, width), BF16),
            pltpu.VMEM((2, BLOCK, 2 * wide), BF16),
            pltpu.VMEM((2 * BLOCK, wide), BF16),
            pltpu.VMEM((8, wide), F32),
            pltpu.VMEM(dwell_map.shape, BF16),
            pltpu.VMEM(target.shape, BF16),
            pltpu.VMEM(bound_mask.shape, jnp.int32),
        ),
        [
            pltpu.VMEM((scen_total, width, width), BF16),
            pltpu.VMEM((2 * BLOCK, width), BF16),
            pltpu.SemaphoreType.DMA((3,)),
        ],
        10**8,
        [SMEM] * 3 + [VMEM] * 2 + [HBM] * 3,
        offsets.T,
        rate_index.reshape(scen_total),
        rate_table,
        row_kernels,
        col_kernels,
        dwell_map,
        target,
        bound_mask,
        limit=None,
    )
    from_dwell, to_outer, to_inner = call(
        functools.partial(send_kernel, blocks),
        "send",
        (
            pltpu.VMEM((tile, wide), BF16),
            pltpu.VMEM((BLOCK, BLOCK), BF16),
            pltpu.VMEM((BLOCK, BLOCK), BF16),
        ),
        [pltpu.VMEM((tile, width), BF16)],
        10**8,
        [VMEM] * (blocks + 4),
        scale,
        fold,
        edge,
        ends,
        dwell_here,
        *neighbours,
    )
    outer_terms = moved(to_outer, outer)
    inner_terms = moved(to_inner, inner)
    partial = call(
        own_kernel,
        "own",
        pltpu.VMEM((tile, BLOCK), F32),
        [
            pltpu.VMEM((tile + 2 * HALF, width), BF16),
            pltpu.VMEM((scen_total * (tile + 2 * BLOCK), BLOCK), BF16),
        ],
        10**9,
        [VMEM] * 7,
        scale,
        fwd,
        adj,
        own,
        from_dwell,
        target_here,
        dwell_here,
    )
    return call(
        finish_kernel,
        "finish",
        jax.ShapeDtypeStruct(dwell_map.shape, BF16),
        [],
        10**6,
        [VMEM] * 4,
        partial,
        bound_here,
        outer_terms,
        inner_terms,
    )


def solution(mesh):
    return jax.shard_map(
        shards,
        mesh=mesh,
        in_specs=(
            P("space", "scen"),
            P("space", None),
            P("space", "scen"),
            P(),
            P(),
            P(),
            P(),
            P(),
        ),
        out_specs=P("space", "scen"),
        check_vma=False,
    )
```

```python
import functools

import jax
import jax.numpy as jnp
from jax import lax
from jax.experimental import pallas as pl
from jax.experimental.pallas import tpu as pltpu
from jax.sharding import PartitionSpec as P

KTAPS = 63
RADIUS = 31
BLOCK = 128
HALF = 64
STEP_SIZE = 1.0
BF16 = jnp.bfloat16
F32 = jnp.float32
SMEM = pl.BlockSpec(memory_space=pltpu.SMEM)
VMEM = pl.BlockSpec(memory_space=pltpu.VMEM)
HBM = pl.BlockSpec(memory_space=pltpu.HBM)


def dot(a, b, contract_b=0):
    return lax.dot_general(
        a, b, (((1,), (contract_b,)), ((), ())), preferred_element_type=F32
    )


def band(line, width):
    lines = jnp.broadcast_to(line[0:1, :width], (BLOCK, width))
    return pltpu.roll(lines, 0, 1, stride=1, stride_axis=0).astype(BF16)


def lanes_of(blocks):
    if blocks == 2:
        own = lax.axis_index("scen") * BLOCK
        return [
            pl.ds(pl.multiple_of(own, BLOCK), BLOCK),
            pl.ds(pl.multiple_of(BLOCK - own, BLOCK), BLOCK),
        ]
    return [pl.ds((blocks - 1) // 2 * BLOCK, BLOCK), pl.ds(0, BLOCK), pl.ds(2 * BLOCK, BLOCK)][:blocks]


def pack_kernel(
    dwell, target, offsets, levels, rates, row_taps, col_taps,
    outer_side, outer_own, lines, scale_ref,
    offsets_here, levels_here, rates_here, rows_here, cols_here, sems,
):
    tile = dwell.shape[0]
    odd = lax.rem(lax.axis_index("space"), 2)
    mine = pl.ds(pl.multiple_of(lax.axis_index("scen") * BLOCK, BLOCK), BLOCK)
    dwell_rows = pl.ds(pl.multiple_of(odd * (tile - BLOCK), BLOCK), BLOCK)
    target_rows = pl.ds(pl.multiple_of(odd * (tile - HALF), HALF), HALF)
    moves = [
        (offsets, offsets_here),
        (levels, levels_here),
        (rates, rates_here),
        (row_taps, rows_here),
        (col_taps, cols_here),
    ]
    for out in (outer_side, outer_own):
        moves.append((dwell.at[dwell_rows, :], out.at[pl.ds(0, BLOCK), :]))
        moves.append((target.at[target_rows, mine], out.at[pl.ds(BLOCK, HALF), :]))
    copies = [pltpu.make_async_copy(a, b, sems.at[i]) for i, (a, b) in enumerate(moves)]
    for copy in copies:
        copy.start()
    turn = (
        lax.broadcasted_iota(jnp.int32, (KTAPS, KTAPS), 0)
        + lax.broadcasted_iota(jnp.int32, (KTAPS, KTAPS), 1)
        == KTAPS - 1
    )
    turn = turn.astype(F32).astype(BF16)
    for copy in copies:
        copy.wait()
    scen_total = lines.shape[0]
    rest = jnp.zeros((rates.shape[0], 3 * BLOCK - KTAPS), F32)
    rows, cols = rows_here[...], cols_here[...]
    tables = [rows.astype(F32), dot(rows, turn), dot(cols, turn)]
    tables = [jnp.concatenate([table, rest], axis=1) for table in tables]
    for s in range(scen_total):
        level = levels_here[s]
        rate = rates_here[level]
        here = slice(s * BLOCK, (s + 1) * BLOCK)
        scale_ref[0:1, here] = jnp.full((1, BLOCK), rate * rate * (1.0 / scen_total), F32)
        scale_ref[1:2, here] = jnp.full((1, BLOCK), rate * (-1.0 / scen_total), F32)
        shift_row, shift_col = offsets_here[0, s], offsets_here[1, s]
        starts = (
            HALF - RADIUS - shift_row,
            HALF - RADIUS + shift_row,
            BLOCK - RADIUS + shift_col,
        )
        for k, (table, start) in enumerate(zip(tables, starts)):
            line = table[0:1]
            for r in range(1, table.shape[0]):
                line = jnp.where(level == r, table[r : r + 1], line)
            lines[s, k] = pltpu.roll(jnp.broadcast_to(line, (8, 3 * BLOCK)), start, 1)


def bands_kernel(lines, fwd_ref, adj_ref, fold_ref, own_ref, edge_ref, col_ref):
    scen_total, width = col_ref.shape[0], col_ref.shape[1]
    blocks = width // BLOCK
    scen = lax.axis_index("scen")
    own_rows = lanes_of(blocks)[0]
    for s in range(scen_total):
        fwd, adj = band(lines[s, 0], 2 * BLOCK), band(lines[s, 1], 2 * BLOCK)
        fwd_ref[s] = fwd
        adj_ref[s] = adj
        upper, lower = adj[:, :BLOCK], adj[:, BLOCK:]
        at = 2 * s * BLOCK
        edge_ref[0, :, at : at + BLOCK] = dot(upper, fwd[:, :BLOCK]).astype(BF16)
        edge_ref[0, :, at + BLOCK : at + 2 * BLOCK] = upper
        edge_ref[1, :, at : at + BLOCK] = dot(lower, fwd[:, BLOCK:]).astype(BF16)
        edge_ref[1, :, at + BLOCK : at + 2 * BLOCK] = lower
        near = band(lines[s, 2], 3 * BLOCK)
        for y in range(blocks):
            for j in range(blocks):
                piece = jnp.zeros((BLOCK, BLOCK), BF16)
                if abs(j - y) <= 1:
                    piece = near[:, (j - y + 1) * BLOCK : (j - y + 2) * BLOCK]
                col_ref[s, y * BLOCK : (y + 1) * BLOCK, j * BLOCK : (j + 1) * BLOCK] = piece
    if blocks > 2:
        for outside, j in ((scen == 0, 0), (scen == lax.axis_size("scen") - 1, 2)):

            @pl.when(outside)
            def _():
                for s in range(scen_total):
                    col_ref[s, :, j * BLOCK : (j + 1) * BLOCK] = jnp.zeros((width, BLOCK), BF16)

    for s in range(scen_total):
        here = slice(s * BLOCK, (s + 1) * BLOCK)
        mine = col_ref[s, own_rows, :]
        own_ref[here, :] = mine
        fold_ref[:, here] = dot(col_ref[s], mine, 1).astype(BF16)


def clear_outside(blocks, ref):
    if blocks > 2:
        scen = lax.axis_index("scen")
        for outside, b in ((scen == 0, 0), (scen == lax.axis_size("scen") - 1, 2)):

            @pl.when(outside)
            def _():
                ref[:, b * BLOCK : (b + 1) * BLOCK] = jnp.zeros((ref.shape[0], BLOCK), BF16)


def terms_of(edge, dwell_rows, target_rows):
    rhs = []
    for s in range(dwell_rows.shape[1] // BLOCK):
        here = slice(s * BLOCK, (s + 1) * BLOCK)
        rhs += [dwell_rows[:, here], target_rows[:, here]]
    return dot(edge, jnp.concatenate(rhs, axis=0))


def send_kernel(blocks, scale, fold, own, edge, target, *refs):
    mids, (from_ref, to_inner, tile_ref, target_ends) = refs[:blocks], refs[blocks:]
    tile = tile_ref.shape[0]
    odd = lax.rem(lax.axis_index("space"), 2)
    for b, lane in enumerate(lanes_of(blocks)):
        tile_ref[:, lane] = mids[b][...]
    clear_outside(blocks, tile_ref)
    from_ref[...] = (dot(tile_ref[...], fold[...]) * scale[0:1, :]).astype(BF16)
    rows = pl.ds(pl.multiple_of((1 - odd) * (tile - HALF), HALF), HALF)
    target_ends[...] = jnp.zeros(target_ends.shape, BF16)
    target_ends[pl.ds(pl.multiple_of(odd * HALF, HALF), HALF), :] = target[rows, :]
    ends = (dot(target_ends[...], own[...], 1) * scale[1:2, :]).astype(BF16)
    rows = pl.ds(pl.multiple_of((1 - odd) * (tile - BLOCK), BLOCK), BLOCK)
    to_inner[...] = terms_of(edge[odd], from_ref[rows, :], ends).astype(BF16)


def own_kernel(scale, fwd, adj, own, from_dwell, target, dwell, partial_ref, target_all, rhs):
    scen_total, width = fwd.shape[0], own.shape[1]
    tile = target.shape[0]
    space = lax.axis_index("space")
    target_all[:HALF, :] = jnp.zeros((HALF, width), BF16)
    target_all[HALF : HALF + tile, :] = target[...]
    target_all[HALF + tile :, :] = jnp.zeros((HALF, width), BF16)
    from_target = (dot(target_all[...], own[...], 1) * scale[1:2, :]).astype(BF16)
    lane = lax.broadcasted_iota(jnp.int32, (BLOCK, 2 * BLOCK), 1)
    cuts = (
        (space == 0) & (lane < HALF),
        (space == lax.axis_size("space") - 1) & (lane >= 2 * BLOCK - HALF),
    )
    for b in range(2):
        lhs = []
        for s in range(scen_total):
            here = slice(s * BLOCK, (s + 1) * BLOCK)
            back = jnp.where(cuts[b], jnp.zeros((BLOCK, 2 * BLOCK), BF16), adj[s])
            upper, lower = dot(back[:, :BLOCK], fwd[s]), dot(back[:, BLOCK:], fwd[s])
            middle = (upper[:, BLOCK:] + lower[:, :BLOCK]).astype(BF16)
            if b == 0:
                lhs += [middle, lower[:, BLOCK:].astype(BF16), back]
            else:
                lhs += [upper[:, :BLOCK].astype(BF16), middle, back]
            at = 4 * s * BLOCK
            rhs[at : at + tile, :] = from_dwell[:, here]
            rhs[at + tile : at + tile + 2 * BLOCK, :] = from_target[b * BLOCK : (b + 2) * BLOCK, here]
        gradient = dot(jnp.concatenate(lhs, axis=1), rhs[...])
        half = slice(b * BLOCK, (b + 1) * BLOCK)
        partial_ref[half, :] = dwell[half, :].astype(F32) - STEP_SIZE * gradient


def finish_kernel(blocks, scale, fold, own, edge, partial, bound, inner, *refs):
    halos, (out, dwell_halo, target_halo) = refs[blocks - 1 : blocks] + refs[: blocks - 1], refs[blocks:]
    tile, width = out.shape[0], own.shape[1]
    space = lax.axis_index("space")
    odd = lax.rem(space, 2)
    goal_rows = pl.ds(pl.multiple_of(odd * HALF, HALF), HALF)
    target_halo[...] = jnp.zeros((BLOCK, width), BF16)
    for b, lane in enumerate(lanes_of(blocks)):
        dwell_halo[:, lane] = halos[b][:BLOCK, :]
        target_halo[goal_rows, lane] = halos[b][BLOCK:, :]
    clear_outside(blocks, dwell_halo)
    clear_outside(blocks, target_halo)
    from_dwell = (dot(dwell_halo[...], fold[...]) * scale[0:1, :]).astype(BF16)
    from_target = (dot(target_halo[...], own[...], 1) * scale[1:2, :]).astype(BF16)
    terms = terms_of(edge[odd], from_dwell, from_target)
    end = (space == 0) | (space == lax.axis_size("space") - 1)
    terms = jnp.where(end, jnp.zeros_like(terms), terms)
    for at, gradient in ((odd, terms), (1 - odd, inner[...].astype(F32))):
        half = pl.ds(pl.multiple_of(at * (tile - BLOCK), BLOCK), BLOCK)
        stepped = partial[half, :] - STEP_SIZE * gradient
        out[half, :] = jnp.where(
            bound[half, :] == 1, jnp.maximum(stepped, 0.0), stepped
        ).astype(BF16)


def shards(
    dwell_map, target_map, bound_mask, offsets, rate_index, rate_table, row_kernels, col_kernels
):
    tile = dwell_map.shape[0]
    n_space, n_scen = lax.axis_size("space"), lax.axis_size("scen")
    scen = lax.axis_index("scen")
    scen_total = offsets.shape[0]
    blocks = min(n_scen, 3)
    width = blocks * BLOCK
    sides = {1: [], 2: [1]}.get(n_scen, [-1, 1])

    def moved(x, partner):
        pairs = []
        for i in range(n_space):
            for j in range(n_scen):
                a, b = partner(i, j)
                pairs.append((a * n_scen + b % n_scen, i * n_scen + j))
        return lax.ppermute(x, ("space", "scen"), pairs)

    def side(cols):
        return lambda i, j: (i, j + cols)

    def inner(i, j):
        return i ^ 1, j

    def outer(cols):
        def partner(i, j):
            if i in (0, n_space - 1):
                return i, (j ^ 1 if n_scen % 2 == 0 else j)
            return ((i - 1) ^ 1) + 1, j + cols

        return partner

    def call(kernel, name, outs, scratch, flops, specs, *args, limit=32 * 1024 * 1024):
        return pl.pallas_call(
            kernel,
            out_shape=outs,
            in_specs=specs,
            out_specs=jax.tree.map(lambda _: VMEM, outs),
            scratch_shapes=scratch,
            compiler_params=pltpu.CompilerParams(vmem_limit_bytes=limit),
            cost_estimate=pl.CostEstimate(
                flops=flops, bytes_accessed=flops // 100, transcendentals=0
            ),
            name=name,
        )(*args)

    if n_scen <= 2:
        target = target_map
    else:
        target = lax.dynamic_slice_in_dim(
            jnp.pad(target_map, ((0, 0), (BLOCK, BLOCK))), scen * BLOCK, width, 1
        )
    neighbours = [moved(dwell_map, side(c)) for c in sides]
    wide = scen_total * BLOCK
    rates = rate_table.shape[0]
    outer_side, outer_own, lines, scale = call(
        pack_kernel,
        "pack",
        (
            pltpu.VMEM((BLOCK + HALF, BLOCK), BF16),
            pltpu.VMEM((BLOCK + HALF, BLOCK), BF16),
            pltpu.VMEM((scen_total, 3, 8, 3 * BLOCK), F32),
            pltpu.VMEM((8, wide), F32),
        ),
        [
            pltpu.SMEM((2, scen_total), jnp.int32),
            pltpu.SMEM((scen_total,), jnp.int32),
            pltpu.SMEM((rates,), F32),
            pltpu.VMEM((rates, KTAPS), BF16),
            pltpu.VMEM((rates, KTAPS), BF16),
            pltpu.SemaphoreType.DMA((9,)),
        ],
        10**5,
        [HBM] * 7,
        dwell_map,
        target_map,
        offsets.T,
        rate_index.reshape(scen_total),
        rate_table,
        row_kernels,
        col_kernels,
        limit=None,
    )
    fwd, adj, fold, own, edge = call(
        bands_kernel,
        "bands",
        (
            pltpu.VMEM((scen_total, BLOCK, 2 * BLOCK), BF16),
            pltpu.VMEM((scen_total, BLOCK, 2 * BLOCK), BF16),
            pltpu.VMEM((width, wide), BF16),
            pltpu.VMEM((wide, width), BF16),
            pltpu.VMEM((2, BLOCK, 2 * wide), BF16),
        ),
        [pltpu.VMEM((scen_total, width, width), BF16)],
        10**8,
        [VMEM],
        lines,
    )
    halos = [moved(outer_side if c else outer_own, outer(c)) for c in [0] + sides]
    from_dwell, to_inner = call(
        functools.partial(send_kernel, blocks),
        "send",
        (pltpu.VMEM((tile, wide), BF16), pltpu.VMEM((BLOCK, BLOCK), BF16)),
        [pltpu.VMEM((tile, width), BF16), pltpu.VMEM((BLOCK, width), BF16)],
        10**8,
        [VMEM] * (blocks + 5),
        scale,
        fold,
        own,
        edge,
        target,
        dwell_map,
        *neighbours,
    )
    inner_terms = moved(to_inner, inner)
    partial = call(
        own_kernel,
        "own",
        pltpu.VMEM((tile, BLOCK), F32),
        [
            pltpu.VMEM((tile + 2 * HALF, width), BF16),
            pltpu.VMEM((scen_total * (tile + 2 * BLOCK), BLOCK), BF16),
        ],
        10**9,
        [VMEM] * 7,
        scale,
        fwd,
        adj,
        own,
        from_dwell,
        target,
        dwell_map,
    )
    return call(
        functools.partial(finish_kernel, blocks),
        "finish",
        jax.ShapeDtypeStruct(dwell_map.shape, BF16),
        [pltpu.VMEM((BLOCK, width), BF16), pltpu.VMEM((BLOCK, width), BF16)],
        10**6,
        [VMEM] * (7 + blocks),
        scale,
        fold,
        own,
        edge,
        partial,
        bound_mask,
        inner_terms,
        *halos[1:],
        halos[0],
    )


def solution(mesh):
    return jax.shard_map(
        shards,
        mesh=mesh,
        in_specs=(
            P("space", "scen"),
            P("space", None),
            P("space", "scen"),
            P(),
            P(),
            P(),
            P(),
            P(),
        ),
        out_specs=P("space", "scen"),
        check_vma=False,
    )
```

```python
import functools

import jax
import jax.numpy as jnp
from jax import lax
from jax.experimental import pallas as pl
from jax.experimental.pallas import tpu as pltpu
from jax.sharding import PartitionSpec as P

KTAPS = 63
RADIUS = 31
BLOCK = 128
HALF = 64
STEP_SIZE = 1.0
BF16 = jnp.bfloat16
F32 = jnp.float32
VMEM = pl.BlockSpec(memory_space=pltpu.VMEM)
HBM = pl.BlockSpec(memory_space=pltpu.HBM)


def dot(a, b, contract_b=0):
    return lax.dot_general(
        a, b, (((1,), (contract_b,)), ((), ())), preferred_element_type=F32
    )


def band(table, level, start, width):
    taps = table[0:1]
    for r in range(1, table.shape[0]):
        taps = jnp.where(level == r, table[r : r + 1], taps)
    line = jnp.concatenate([taps, jnp.zeros((1, width - KTAPS), F32)], axis=1)
    line = pltpu.roll(jnp.broadcast_to(line, (8, width)), start, 1)
    lines = jnp.broadcast_to(line[0:1], (BLOCK, width))
    return pltpu.roll(lines, 0, 1, stride=1, stride_axis=0).astype(BF16)


def number(one):
    return jnp.max(one.astype(F32)).astype(jnp.int32)


def lanes_of(blocks):
    if blocks == 2:
        own = lax.axis_index("scen") * BLOCK
        return [
            pl.ds(pl.multiple_of(own, BLOCK), BLOCK),
            pl.ds(pl.multiple_of(BLOCK - own, BLOCK), BLOCK),
        ]
    return [pl.ds((blocks - 1) // 2 * BLOCK, BLOCK), pl.ds(0, BLOCK), pl.ds(2 * BLOCK, BLOCK)][:blocks]


def bands_kernel(
    offsets, levels, rates, row_taps, col_taps,
    fwd_ref, adj_ref, fold_ref, own_ref, edge_ref, scale_ref, col_ref,
):
    scen_total, width = col_ref.shape[0], col_ref.shape[1]
    blocks = width // BLOCK
    scen = lax.axis_index("scen")
    own_rows = lanes_of(blocks)[0]
    turn = (
        lax.broadcasted_iota(jnp.int32, (KTAPS, KTAPS), 0)
        + lax.broadcasted_iota(jnp.int32, (KTAPS, KTAPS), 1)
        == KTAPS - 1
    )
    turn = turn.astype(F32).astype(BF16)
    rows, cols = row_taps[...], col_taps[...]
    rows_turned, cols_turned = dot(rows, turn), dot(cols, turn)
    rows = rows.astype(F32)

    for s in range(scen_total):
        level = levels[0:1, s : s + 1]
        rate = rates[0:1, 0:1]
        for r in range(1, rates.shape[1]):
            rate = jnp.where(level == r, rates[0:1, r : r + 1], rate)
        here = slice(s * BLOCK, (s + 1) * BLOCK)
        scale_ref[0:1, here] = jnp.broadcast_to(rate * rate * (1.0 / scen_total), (1, BLOCK))
        scale_ref[1:2, here] = jnp.broadcast_to(rate * (-1.0 / scen_total), (1, BLOCK))
        shift_row, shift_col = [number(offsets[k : k + 1, s : s + 1]) for k in range(2)]
        fwd = band(rows, level, HALF - RADIUS - shift_row, 2 * BLOCK)
        adj = band(rows_turned, level, HALF - RADIUS + shift_row, 2 * BLOCK)
        fwd_ref[s] = fwd
        adj_ref[s] = adj
        upper, lower = adj[:, :BLOCK], adj[:, BLOCK:]
        at = 2 * s * BLOCK
        edge_ref[0, :, at : at + BLOCK] = dot(upper, fwd[:, :BLOCK]).astype(BF16)
        edge_ref[0, :, at + BLOCK : at + 2 * BLOCK] = upper
        edge_ref[1, :, at : at + BLOCK] = dot(lower, fwd[:, BLOCK:]).astype(BF16)
        edge_ref[1, :, at + BLOCK : at + 2 * BLOCK] = lower
        near = band(cols_turned, level, BLOCK - RADIUS + shift_col, 3 * BLOCK)
        for y in range(blocks):
            for j in range(blocks):
                piece = jnp.zeros((BLOCK, BLOCK), BF16)
                if abs(j - y) <= 1:
                    piece = near[:, (j - y + 1) * BLOCK : (j - y + 2) * BLOCK]
                col_ref[s, y * BLOCK : (y + 1) * BLOCK, j * BLOCK : (j + 1) * BLOCK] = piece
    if blocks > 2:
        for outside, j in ((scen == 0, 0), (scen == lax.axis_size("scen") - 1, 2)):

            @pl.when(outside)
            def _():
                for s in range(scen_total):
                    col_ref[s, :, j * BLOCK : (j + 1) * BLOCK] = jnp.zeros((width, BLOCK), BF16)

    for s in range(scen_total):
        here = slice(s * BLOCK, (s + 1) * BLOCK)
        mine = col_ref[s, own_rows, :]
        own_ref[here, :] = mine
        fold_ref[:, here] = dot(col_ref[s], mine, 1).astype(BF16)


def pack_kernel(dwell, target, *refs):
    small, (out, *small_out), sems = refs[:5], refs[5:11], refs[11]
    tile = dwell.shape[0]
    odd = lax.rem(lax.axis_index("space"), 2)
    mine = pl.ds(pl.multiple_of(lax.axis_index("scen") * BLOCK, BLOCK), BLOCK)
    dwell_rows = pl.ds(pl.multiple_of(odd * (tile - BLOCK), BLOCK), BLOCK)
    target_rows = pl.ds(pl.multiple_of(odd * (tile - HALF), HALF), HALF)
    moves = [
        (dwell.at[dwell_rows, :], out.at[pl.ds(0, BLOCK), :]),
        (target.at[target_rows, mine], out.at[pl.ds(BLOCK, HALF), :]),
        *zip(small, small_out),
    ]
    copies = [pltpu.make_async_copy(a, b, sems.at[i]) for i, (a, b) in enumerate(moves)]
    for copy in copies:
        copy.start()
    for copy in copies:
        copy.wait()


def clear_outside(blocks, ref):
    if blocks > 2:
        scen = lax.axis_index("scen")
        for outside, b in ((scen == 0, 0), (scen == lax.axis_size("scen") - 1, 2)):

            @pl.when(outside)
            def _():
                ref[:, b * BLOCK : (b + 1) * BLOCK] = jnp.zeros((ref.shape[0], BLOCK), BF16)


def terms_of(edge, dwell_rows, target_rows):
    rhs = []
    for s in range(dwell_rows.shape[1] // BLOCK):
        here = slice(s * BLOCK, (s + 1) * BLOCK)
        rhs += [dwell_rows[:, here], target_rows[:, here]]
    return dot(edge, jnp.concatenate(rhs, axis=0))


def send_kernel(blocks, scale, fold, own, edge, target, *refs):
    mids, (from_ref, to_inner, tile_ref, target_ends) = refs[:blocks], refs[blocks:]
    tile = tile_ref.shape[0]
    odd = lax.rem(lax.axis_index("space"), 2)
    for b, lane in enumerate(lanes_of(blocks)):
        tile_ref[:, lane] = mids[b][...]
    clear_outside(blocks, tile_ref)
    from_ref[...] = (dot(tile_ref[...], fold[...]) * scale[0:1, :]).astype(BF16)
    rows = pl.ds(pl.multiple_of((1 - odd) * (tile - HALF), HALF), HALF)
    target_ends[...] = jnp.zeros(target_ends.shape, BF16)
    target_ends[pl.ds(pl.multiple_of(odd * HALF, HALF), HALF), :] = target[rows, :]
    ends = (dot(target_ends[...], own[...], 1) * scale[1:2, :]).astype(BF16)
    rows = pl.ds(pl.multiple_of((1 - odd) * (tile - BLOCK), BLOCK), BLOCK)
    to_inner[...] = terms_of(edge[odd], from_ref[rows, :], ends).astype(BF16)


def own_kernel(scale, fwd, adj, own, from_dwell, target, dwell, partial_ref, target_all, rhs):
    scen_total, width = fwd.shape[0], own.shape[1]
    tile = target.shape[0]
    space = lax.axis_index("space")
    target_all[:HALF, :] = jnp.zeros((HALF, width), BF16)
    target_all[HALF : HALF + tile, :] = target[...]
    target_all[HALF + tile :, :] = jnp.zeros((HALF, width), BF16)
    from_target = (dot(target_all[...], own[...], 1) * scale[1:2, :]).astype(BF16)
    lane = lax.broadcasted_iota(jnp.int32, (BLOCK, 2 * BLOCK), 1)
    cuts = (
        (space == 0) & (lane < HALF),
        (space == lax.axis_size("space") - 1) & (lane >= 2 * BLOCK - HALF),
    )
    for b in range(2):
        lhs = []
        for s in range(scen_total):
            here = slice(s * BLOCK, (s + 1) * BLOCK)
            back = jnp.where(cuts[b], jnp.zeros((BLOCK, 2 * BLOCK), BF16), adj[s])
            upper, lower = dot(back[:, :BLOCK], fwd[s]), dot(back[:, BLOCK:], fwd[s])
            middle = (upper[:, BLOCK:] + lower[:, :BLOCK]).astype(BF16)
            if b == 0:
                lhs += [middle, lower[:, BLOCK:].astype(BF16), back]
            else:
                lhs += [upper[:, :BLOCK].astype(BF16), middle, back]
            at = 4 * s * BLOCK
            rhs[at : at + tile, :] = from_dwell[:, here]
            rhs[at + tile : at + tile + 2 * BLOCK, :] = from_target[b * BLOCK : (b + 2) * BLOCK, here]
        gradient = dot(jnp.concatenate(lhs, axis=1), rhs[...])
        half = slice(b * BLOCK, (b + 1) * BLOCK)
        partial_ref[half, :] = dwell[half, :].astype(F32) - STEP_SIZE * gradient


def finish_kernel(blocks, scale, fold, own, edge, partial, bound, inner, *refs):
    halos, refs = refs[blocks - 1 : blocks] + refs[: blocks - 1], refs[blocks:]
    out, dwell_halo, target_halo, terms = refs
    tile, width = out.shape[0], own.shape[1]
    space = lax.axis_index("space")
    odd = lax.rem(space, 2)
    end = (space == 0) | (space == lax.axis_size("space") - 1)

    def step(at, gradient):
        half = pl.ds(pl.multiple_of(at * (tile - BLOCK), BLOCK), BLOCK)
        stepped = partial[half, :] - STEP_SIZE * gradient
        out[half, :] = jnp.where(
            bound[half, :] == 1, jnp.maximum(stepped, 0.0), stepped
        ).astype(BF16)

    @pl.when(end)
    def _():
        terms[...] = jnp.zeros(terms.shape, F32)

    @pl.when(jnp.logical_not(end))
    def _():
        goal_rows = pl.ds(pl.multiple_of(odd * HALF, HALF), HALF)
        target_halo[...] = jnp.zeros((BLOCK, width), BF16)
        for b, lane in enumerate(lanes_of(blocks)):
            dwell_halo[:, lane] = halos[b][:BLOCK, :]
            target_halo[goal_rows, lane] = halos[b][BLOCK:, :]
        clear_outside(blocks, dwell_halo)
        clear_outside(blocks, target_halo)
        from_dwell = (dot(dwell_halo[...], fold[...]) * scale[0:1, :]).astype(BF16)
        from_target = (dot(target_halo[...], own[...], 1) * scale[1:2, :]).astype(BF16)
        terms[...] = terms_of(edge[odd], from_dwell, from_target)

    step(1 - odd, inner[...].astype(F32))
    step(odd, terms[...])


def shards(
    dwell_map, target_map, bound_mask, offsets, rate_index, rate_table, row_kernels, col_kernels
):
    tile = dwell_map.shape[0]
    n_space, n_scen = lax.axis_size("space"), lax.axis_size("scen")
    scen = lax.axis_index("scen")
    scen_total = offsets.shape[0]
    blocks = min(n_scen, 3)
    width = blocks * BLOCK
    sides = {1: [], 2: [1]}.get(n_scen, [-1, 1])

    def moved(x, partner):
        pairs = []
        for i in range(n_space):
            for j in range(n_scen):
                a, b = partner(i, j)
                pairs.append((a * n_scen + b % n_scen, i * n_scen + j))
        return lax.ppermute(x, ("space", "scen"), pairs)

    def side(cols):
        return lambda i, j: (i, j + cols)

    def inner(i, j):
        return i ^ 1, j

    def outer(cols):
        def partner(i, j):
            if i in (0, n_space - 1):
                return i, (j ^ 1 if n_scen % 2 == 0 else j)
            return ((i - 1) ^ 1) + 1, j + cols

        return partner

    def call(kernel, name, outs, scratch, flops, specs, *args, limit=32 * 1024 * 1024):
        return pl.pallas_call(
            kernel,
            out_shape=outs,
            in_specs=specs,
            out_specs=jax.tree.map(lambda _: VMEM, outs),
            scratch_shapes=scratch,
            compiler_params=pltpu.CompilerParams(vmem_limit_bytes=limit),
            cost_estimate=pl.CostEstimate(
                flops=flops, bytes_accessed=flops // 100, transcendentals=0
            ),
            name=name,
        )(*args)

    if n_scen <= 2:
        target = target_map
    else:
        target = lax.dynamic_slice_in_dim(
            jnp.pad(target_map, ((0, 0), (BLOCK, BLOCK))), scen * BLOCK, width, 1
        )
    neighbours = [moved(dwell_map, side(c)) for c in sides]
    wide = scen_total * BLOCK
    small = (
        offsets.T,
        rate_index.reshape(1, scen_total),
        rate_table.reshape(1, rate_table.shape[0]),
        row_kernels,
        col_kernels,
    )
    to_outer, *small = call(
        pack_kernel,
        "pack",
        (
            pltpu.VMEM((BLOCK + HALF, BLOCK), BF16),
            *(pltpu.VMEM(x.shape, x.dtype) for x in small),
        ),
        [pltpu.SemaphoreType.DMA((7,))],
        10**5,
        [HBM] * 7,
        dwell_map,
        target_map,
        *small,
        limit=None,
    )
    halos = [moved(to_outer, outer(c)) for c in [0] + sides]
    fwd, adj, fold, own, edge, scale = call(
        bands_kernel,
        "bands",
        (
            pltpu.VMEM((scen_total, BLOCK, 2 * BLOCK), BF16),
            pltpu.VMEM((scen_total, BLOCK, 2 * BLOCK), BF16),
            pltpu.VMEM((width, wide), BF16),
            pltpu.VMEM((wide, width), BF16),
            pltpu.VMEM((2, BLOCK, 2 * wide), BF16),
            pltpu.VMEM((8, wide), F32),
        ),
        [
            pltpu.VMEM((scen_total, width, width), BF16),
        ],
        10**8,
        [VMEM] * 5,
        *small,
    )
    from_dwell, to_inner = call(
        functools.partial(send_kernel, blocks),
        "send",
        (pltpu.VMEM((tile, wide), BF16), pltpu.VMEM((BLOCK, BLOCK), BF16)),
        [pltpu.VMEM((tile, width), BF16), pltpu.VMEM((BLOCK, width), BF16)],
        10**8,
        [VMEM] * (blocks + 5),
        scale,
        fold,
        own,
        edge,
        target,
        dwell_map,
        *neighbours,
    )
    inner_terms = moved(to_inner, inner)
    partial = call(
        own_kernel,
        "own",
        pltpu.VMEM((tile, BLOCK), F32),
        [
            pltpu.VMEM((tile + 2 * HALF, width), BF16),
            pltpu.VMEM((scen_total * (tile + 2 * BLOCK), BLOCK), BF16),
        ],
        10**9,
        [VMEM] * 7,
        scale,
        fwd,
        adj,
        own,
        from_dwell,
        target,
        dwell_map,
    )
    return call(
        functools.partial(finish_kernel, blocks),
        "finish",
        jax.ShapeDtypeStruct(dwell_map.shape, BF16),
        [
            pltpu.VMEM((BLOCK, width), BF16),
            pltpu.VMEM((BLOCK, width), BF16),
            pltpu.VMEM((BLOCK, BLOCK), F32),
        ],
        10**6,
        [VMEM] * (7 + blocks),
        scale,
        fold,
        own,
        edge,
        partial,
        bound_mask,
        inner_terms,
        *halos[1:],
        halos[0],
    )


def solution(mesh):
    return jax.shard_map(
        shards,
        mesh=mesh,
        in_specs=(
            P("space", "scen"),
            P("space", None),
            P("space", "scen"),
            P(),
            P(),
            P(),
            P(),
            P(),
        ),
        out_specs=P("space", "scen"),
        check_vma=False,
    )
```

```python
import functools

import jax
import jax.numpy as jnp
from jax import lax
from jax.experimental import pallas as pl
from jax.experimental.pallas import tpu as pltpu
from jax.sharding import PartitionSpec as P

KTAPS = 63
RADIUS = 31
BLOCK = 128
HALF = 64
STEP_SIZE = 1.0
BF16 = jnp.bfloat16
F32 = jnp.float32
VMEM = pl.BlockSpec(memory_space=pltpu.VMEM)
HBM = pl.BlockSpec(memory_space=pltpu.HBM)


def dot(a, b):
    return jnp.dot(a, b, preferred_element_type=F32)


def band(table, level, start, width):
    taps = table[0:1]
    for r in range(1, table.shape[0]):
        taps = jnp.where(level == r, table[r : r + 1], taps)
    line = jnp.concatenate([taps, jnp.zeros((1, width - KTAPS), F32)], axis=1)
    line = pltpu.roll(jnp.broadcast_to(line, (8, width)), start, 1)
    lines = jnp.broadcast_to(line[0:1], (BLOCK, width))
    return pltpu.roll(lines, 0, 1, stride=1, stride_axis=0).astype(BF16)


def number(one):
    return jnp.max(one.astype(F32)).astype(jnp.int32)


def lanes_of(blocks):
    if blocks == 2:
        own = lax.axis_index("scen") * BLOCK
        return [
            pl.ds(pl.multiple_of(own, BLOCK), BLOCK),
            pl.ds(pl.multiple_of(BLOCK - own, BLOCK), BLOCK),
        ]
    return [pl.ds((blocks - 1) // 2 * BLOCK, BLOCK), pl.ds(0, BLOCK), pl.ds(2 * BLOCK, BLOCK)][:blocks]


def bands_kernel(
    offsets, levels, rates, row_taps, col_taps,
    fwd_ref, adj_ref, fold_ref, own_ref, edge_ref, scale_ref, col_ref,
):
    scen_total, width = col_ref.shape[0], col_ref.shape[1]
    blocks = width // BLOCK
    scen = lax.axis_index("scen")
    own_rows = lanes_of(blocks)[0]
    turn = (
        lax.broadcasted_iota(jnp.int32, (KTAPS, KTAPS), 0)
        + lax.broadcasted_iota(jnp.int32, (KTAPS, KTAPS), 1)
        == KTAPS - 1
    )
    turn = turn.astype(F32).astype(BF16)
    rows, cols = row_taps[...], col_taps[...]
    rows_turned, cols_turned = dot(rows, turn), dot(cols, turn)
    rows = rows.astype(F32)

    for s in range(scen_total):
        level = levels[0:1, s : s + 1]
        rate = rates[0:1, 0:1]
        for r in range(1, rates.shape[1]):
            rate = jnp.where(level == r, rates[0:1, r : r + 1], rate)
        here = slice(s * BLOCK, (s + 1) * BLOCK)
        scale_ref[0:1, here] = jnp.broadcast_to(rate * rate * (1.0 / scen_total), (1, BLOCK))
        scale_ref[1:2, here] = jnp.broadcast_to(rate * (-1.0 / scen_total), (1, BLOCK))
        shift_row, shift_col = [number(offsets[k : k + 1, s : s + 1]) for k in range(2)]
        fwd = band(rows, level, HALF - RADIUS - shift_row, 2 * BLOCK)
        adj = band(rows_turned, level, HALF - RADIUS + shift_row, 2 * BLOCK)
        fwd_ref[s] = fwd
        adj_ref[s] = adj
        upper, lower = adj[:, :BLOCK], adj[:, BLOCK:]
        at = 2 * s * BLOCK
        edge_ref[0, :, at : at + BLOCK] = dot(upper, fwd[:, :BLOCK]).astype(BF16)
        edge_ref[0, :, at + BLOCK : at + 2 * BLOCK] = upper
        edge_ref[1, :, at : at + BLOCK] = dot(lower, fwd[:, BLOCK:]).astype(BF16)
        edge_ref[1, :, at + BLOCK : at + 2 * BLOCK] = lower
        near = band(cols_turned, level, BLOCK - RADIUS + shift_col, 3 * BLOCK)
        for y in range(blocks):
            for j in range(blocks):
                piece = jnp.zeros((BLOCK, BLOCK), BF16)
                if abs(j - y) <= 1:
                    piece = near[:, (j - y + 1) * BLOCK : (j - y + 2) * BLOCK]
                col_ref[s, y * BLOCK : (y + 1) * BLOCK, j * BLOCK : (j + 1) * BLOCK] = piece
    if blocks > 2:
        for outside, j in ((scen == 0, 0), (scen == lax.axis_size("scen") - 1, 2)):

            @pl.when(outside)
            def _():
                for s in range(scen_total):
                    col_ref[s, :, j * BLOCK : (j + 1) * BLOCK] = jnp.zeros((width, BLOCK), BF16)

    for s in range(scen_total):
        here = slice(s * BLOCK, (s + 1) * BLOCK)
        mine = col_ref[s, own_rows, :].T
        own_ref[:, here] = mine
        fold_ref[:, here] = dot(col_ref[s], mine).astype(BF16)


def pack_kernel(dwell, target, *refs):
    small, (out, *small_out), sems = refs[:5], refs[5:11], refs[11]
    tile = dwell.shape[0]
    odd = lax.rem(lax.axis_index("space"), 2)
    mine = pl.ds(pl.multiple_of(lax.axis_index("scen") * BLOCK, BLOCK), BLOCK)
    dwell_rows = pl.ds(pl.multiple_of(odd * (tile - BLOCK), BLOCK), BLOCK)
    target_rows = pl.ds(pl.multiple_of(odd * (tile - HALF), HALF), HALF)
    moves = [
        (dwell.at[dwell_rows, :], out.at[pl.ds(0, BLOCK), :]),
        (target.at[target_rows, mine], out.at[pl.ds(BLOCK, HALF), :]),
        *zip(small, small_out),
    ]
    copies = [pltpu.make_async_copy(a, b, sems.at[i]) for i, (a, b) in enumerate(moves)]
    for copy in copies:
        copy.start()
    for copy in copies:
        copy.wait()


def clear_outside(blocks, ref):
    if blocks > 2:
        scen = lax.axis_index("scen")
        for outside, b in ((scen == 0, 0), (scen == lax.axis_size("scen") - 1, 2)):

            @pl.when(outside)
            def _():
                ref[:, b * BLOCK : (b + 1) * BLOCK] = jnp.zeros((ref.shape[0], BLOCK), BF16)


def terms_of(edge, dwell_rows, target_rows):
    rhs = []
    for s in range(dwell_rows.shape[1] // BLOCK):
        here = slice(s * BLOCK, (s + 1) * BLOCK)
        rhs += [dwell_rows[:, here], target_rows[:, here]]
    return dot(edge, jnp.concatenate(rhs, axis=0))


def send_kernel(blocks, scale, fold, own, edge, target, *refs):
    mids, (from_ref, to_inner, tile_ref, target_ends) = refs[:blocks], refs[blocks:]
    tile = tile_ref.shape[0]
    odd = lax.rem(lax.axis_index("space"), 2)
    for b, lane in enumerate(lanes_of(blocks)):
        tile_ref[:, lane] = mids[b][...]
    clear_outside(blocks, tile_ref)
    from_ref[...] = (dot(tile_ref[...], fold[...]) * scale[0:1, :]).astype(BF16)
    rows = pl.ds(pl.multiple_of((1 - odd) * (tile - HALF), HALF), HALF)
    target_ends[...] = jnp.zeros(target_ends.shape, BF16)
    target_ends[pl.ds(pl.multiple_of(odd * HALF, HALF), HALF), :] = target[rows, :]
    ends = (dot(target_ends[...], own[...]) * scale[1:2, :]).astype(BF16)
    rows = pl.ds(pl.multiple_of((1 - odd) * (tile - BLOCK), BLOCK), BLOCK)
    to_inner[...] = terms_of(edge[odd], from_ref[rows, :], ends).astype(BF16)


def own_kernel(scale, fwd, adj, own, from_dwell, target, dwell, partial_ref, target_all, rhs):
    scen_total, width = fwd.shape[0], own.shape[0]
    tile = target.shape[0]
    space = lax.axis_index("space")
    target_all[:HALF, :] = jnp.zeros((HALF, width), BF16)
    target_all[HALF : HALF + tile, :] = target[...]
    target_all[HALF + tile :, :] = jnp.zeros((HALF, width), BF16)
    from_target = (dot(target_all[...], own[...]) * scale[1:2, :]).astype(BF16)
    lane = lax.broadcasted_iota(jnp.int32, (BLOCK, 2 * BLOCK), 1)
    cuts = (
        (space == 0) & (lane < HALF),
        (space == lax.axis_size("space") - 1) & (lane >= 2 * BLOCK - HALF),
    )
    for b in range(2):
        lhs = []
        for s in range(scen_total):
            here = slice(s * BLOCK, (s + 1) * BLOCK)
            back = jnp.where(cuts[b], jnp.zeros((BLOCK, 2 * BLOCK), BF16), adj[s])
            upper, lower = dot(back[:, :BLOCK], fwd[s]), dot(back[:, BLOCK:], fwd[s])
            middle = (upper[:, BLOCK:] + lower[:, :BLOCK]).astype(BF16)
            if b == 0:
                lhs += [middle, lower[:, BLOCK:].astype(BF16), back]
            else:
                lhs += [upper[:, :BLOCK].astype(BF16), middle, back]
            at = 4 * s * BLOCK
            rhs[at : at + tile, :] = from_dwell[:, here]
            rhs[at + tile : at + tile + 2 * BLOCK, :] = from_target[b * BLOCK : (b + 2) * BLOCK, here]
        gradient = dot(jnp.concatenate(lhs, axis=1), rhs[...])
        half = slice(b * BLOCK, (b + 1) * BLOCK)
        partial_ref[half, :] = dwell[half, :].astype(F32) - STEP_SIZE * gradient


def finish_kernel(blocks, scale, fold, own, edge, partial, bound, inner, *refs):
    halos, refs = refs[blocks - 1 : blocks] + refs[: blocks - 1], refs[blocks:]
    out, dwell_halo, target_halo = refs
    tile, width = out.shape[0], own.shape[0]
    space = lax.axis_index("space")
    odd = lax.rem(space, 2)
    end = (space == 0) | (space == lax.axis_size("space") - 1)

    def step(at, gradient):
        half = pl.ds(pl.multiple_of(at * (tile - BLOCK), BLOCK), BLOCK)
        stepped = partial[half, :] - STEP_SIZE * gradient
        out[half, :] = jnp.where(
            bound[half, :] == 1, jnp.maximum(stepped, 0.0), stepped
        ).astype(BF16)

    @pl.when(end)
    def _():
        step(1 - odd, inner[...].astype(F32))
        step(odd, 0.0)

    @pl.when(jnp.logical_not(end))
    def _():
        goal_rows = pl.ds(pl.multiple_of(odd * HALF, HALF), HALF)
        target_halo[...] = jnp.zeros((BLOCK, width), BF16)
        for b, lane in enumerate(lanes_of(blocks)):
            dwell_halo[:, lane] = halos[b][:BLOCK, :]
            target_halo[goal_rows, lane] = halos[b][BLOCK:, :]
        clear_outside(blocks, dwell_halo)
        clear_outside(blocks, target_halo)
        from_dwell = (dot(dwell_halo[...], fold[...]) * scale[0:1, :]).astype(BF16)
        from_target = (dot(target_halo[...], own[...]) * scale[1:2, :]).astype(BF16)
        terms = terms_of(edge[odd], from_dwell, from_target)
        step(1 - odd, inner[...].astype(F32))
        step(odd, terms)


def shards(
    dwell_map, target_map, bound_mask, offsets, rate_index, rate_table, row_kernels, col_kernels
):
    tile = dwell_map.shape[0]
    n_space, n_scen = lax.axis_size("space"), lax.axis_size("scen")
    scen = lax.axis_index("scen")
    scen_total = offsets.shape[0]
    blocks = min(n_scen, 3)
    width = blocks * BLOCK
    sides = {1: [], 2: [1]}.get(n_scen, [-1, 1])

    def moved(x, partner):
        pairs = []
        for i in range(n_space):
            for j in range(n_scen):
                a, b = partner(i, j)
                pairs.append((a * n_scen + b % n_scen, i * n_scen + j))
        return lax.ppermute(x, ("space", "scen"), pairs)

    def side(cols):
        return lambda i, j: (i, j + cols)

    def inner(i, j):
        return i ^ 1, j

    def outer(cols):
        def partner(i, j):
            if i in (0, n_space - 1):
                return i, (j ^ 1 if n_scen % 2 == 0 else j)
            return ((i - 1) ^ 1) + 1, j + cols

        return partner

    def call(kernel, name, outs, scratch, flops, specs, *args, limit=32 * 1024 * 1024):
        return pl.pallas_call(
            kernel,
            out_shape=outs,
            in_specs=specs,
            out_specs=jax.tree.map(lambda _: VMEM, outs),
            scratch_shapes=scratch,
            compiler_params=pltpu.CompilerParams(vmem_limit_bytes=limit),
            cost_estimate=pl.CostEstimate(
                flops=flops, bytes_accessed=flops // 100, transcendentals=0
            ),
            name=name,
        )(*args)

    if n_scen <= 2:
        target = target_map
    else:
        target = lax.dynamic_slice_in_dim(
            jnp.pad(target_map, ((0, 0), (BLOCK, BLOCK))), scen * BLOCK, width, 1
        )
    neighbours = [moved(dwell_map, side(c)) for c in sides]
    wide = scen_total * BLOCK
    small = (
        offsets.T,
        rate_index.reshape(1, scen_total),
        rate_table.reshape(1, rate_table.shape[0]),
        row_kernels,
        col_kernels,
    )
    to_outer, *small = call(
        pack_kernel,
        "pack",
        (
            pltpu.VMEM((BLOCK + HALF, BLOCK), BF16),
            *(pltpu.VMEM(x.shape, x.dtype) for x in small),
        ),
        [pltpu.SemaphoreType.DMA((7,))],
        10**5,
        [HBM] * 7,
        dwell_map,
        target_map,
        *small,
        limit=None,
    )
    halos = [moved(to_outer, outer(c)) for c in [0] + sides]
    fwd, adj, fold, own, edge, scale = call(
        bands_kernel,
        "bands",
        (
            pltpu.VMEM((scen_total, BLOCK, 2 * BLOCK), BF16),
            pltpu.VMEM((scen_total, BLOCK, 2 * BLOCK), BF16),
            pltpu.VMEM((width, wide), BF16),
            pltpu.VMEM((width, wide), BF16),
            pltpu.VMEM((2, BLOCK, 2 * wide), BF16),
            pltpu.VMEM((8, wide), F32),
        ),
        [
            pltpu.VMEM((scen_total, width, width), BF16),
        ],
        10**8,
        [VMEM] * 5,
        *small,
    )
    from_dwell, to_inner = call(
        functools.partial(send_kernel, blocks),
        "send",
        (pltpu.VMEM((tile, wide), BF16), pltpu.VMEM((BLOCK, BLOCK), BF16)),
        [pltpu.VMEM((tile, width), BF16), pltpu.VMEM((BLOCK, width), BF16)],
        10**8,
        [VMEM] * (blocks + 5),
        scale,
        fold,
        own,
        edge,
        target,
        dwell_map,
        *neighbours,
    )
    inner_terms = moved(to_inner, inner)
    partial = call(
        own_kernel,
        "own",
        pltpu.VMEM((tile, BLOCK), F32),
        [
            pltpu.VMEM((tile + 2 * HALF, width), BF16),
            pltpu.VMEM((scen_total * (tile + 2 * BLOCK), BLOCK), BF16),
        ],
        10**9,
        [VMEM] * 7,
        scale,
        fwd,
        adj,
        own,
        from_dwell,
        target,
        dwell_map,
    )
    return call(
        functools.partial(finish_kernel, blocks),
        "finish",
        jax.ShapeDtypeStruct(dwell_map.shape, BF16),
        [pltpu.VMEM((BLOCK, width), BF16), pltpu.VMEM((BLOCK, width), BF16)],
        10**6,
        [VMEM] * (7 + blocks),
        scale,
        fold,
        own,
        edge,
        partial,
        bound_mask,
        inner_terms,
        *halos[1:],
        halos[0],
    )


def solution(mesh):
    return jax.shard_map(
        shards,
        mesh=mesh,
        in_specs=(
            P("space", "scen"),
            P("space", None),
            P("space", "scen"),
            P(),
            P(),
            P(),
            P(),
            P(),
        ),
        out_specs=P("space", "scen"),
        check_vma=False,
    )
```

```python
import functools

import jax
import jax.numpy as jnp
from jax import lax
from jax.experimental import pallas as pl
from jax.experimental.pallas import tpu as pltpu
from jax.sharding import PartitionSpec as P

KTAPS = 63
RADIUS = 31
BLOCK = 128
HALF = 64
STEP_SIZE = 1.0
BF16 = jnp.bfloat16
F32 = jnp.float32
VMEM = pl.BlockSpec(memory_space=pltpu.VMEM)
HBM = pl.BlockSpec(memory_space=pltpu.HBM)


def dot(a, b):
    return jnp.dot(a, b, preferred_element_type=F32)


def band(table, level, start, width):
    taps = table[0:1]
    for r in range(1, table.shape[0]):
        taps = jnp.where(level == r, table[r : r + 1], taps)
    line = jnp.concatenate([taps, jnp.zeros((1, width - KTAPS), F32)], axis=1)
    line = pltpu.roll(jnp.broadcast_to(line, (8, width)), start, 1)
    lines = jnp.broadcast_to(line[0:1], (BLOCK, width))
    return pltpu.roll(lines, 0, 1, stride=1, stride_axis=0).astype(BF16)


def number(one):
    return jnp.max(one.astype(F32)).astype(jnp.int32)


def lanes_of(blocks):
    if blocks == 2:
        own = lax.axis_index("scen") * BLOCK
        return [
            pl.ds(pl.multiple_of(own, BLOCK), BLOCK),
            pl.ds(pl.multiple_of(BLOCK - own, BLOCK), BLOCK),
        ]
    return [pl.ds((blocks - 1) // 2 * BLOCK, BLOCK), pl.ds(0, BLOCK), pl.ds(2 * BLOCK, BLOCK)][:blocks]


def bands_kernel(
    offsets, levels, rates, row_taps, col_taps,
    fwd_ref, adj_ref, fold_ref, own_ref, edge_ref, scale_ref, col_ref,
):
    scen_total, width = col_ref.shape[0], col_ref.shape[1]
    blocks = width // BLOCK
    scen = lax.axis_index("scen")
    own_rows = lanes_of(blocks)[0]
    turn = (
        lax.broadcasted_iota(jnp.int32, (KTAPS, KTAPS), 0)
        + lax.broadcasted_iota(jnp.int32, (KTAPS, KTAPS), 1)
        == KTAPS - 1
    )
    turn = turn.astype(F32).astype(BF16)
    rows, cols = row_taps[...], col_taps[...]
    rows_turned, cols_turned = dot(rows, turn), dot(cols, turn)
    rows = rows.astype(F32)

    for s in range(scen_total):
        level = levels[0:1, s : s + 1]
        rate = rates[0:1, 0:1]
        for r in range(1, rates.shape[1]):
            rate = jnp.where(level == r, rates[0:1, r : r + 1], rate)
        here = slice(s * BLOCK, (s + 1) * BLOCK)
        scale_ref[0:1, here] = jnp.broadcast_to(rate * rate * (1.0 / scen_total), (1, BLOCK))
        scale_ref[1:2, here] = jnp.broadcast_to(rate * (-1.0 / scen_total), (1, BLOCK))
        shift_row, shift_col = [number(offsets[k : k + 1, s : s + 1]) for k in range(2)]
        fwd = band(rows, level, HALF - RADIUS - shift_row, 2 * BLOCK)
        adj = band(rows_turned, level, HALF - RADIUS + shift_row, 2 * BLOCK)
        fwd_ref[s] = fwd
        adj_ref[s] = adj
        upper, lower = adj[:, :BLOCK], adj[:, BLOCK:]
        at = 2 * s * BLOCK
        edge_ref[0, :, at : at + BLOCK] = dot(upper, fwd[:, :BLOCK]).astype(BF16)
        edge_ref[0, :, at + BLOCK : at + 2 * BLOCK] = upper
        edge_ref[1, :, at : at + BLOCK] = dot(lower, fwd[:, BLOCK:]).astype(BF16)
        edge_ref[1, :, at + BLOCK : at + 2 * BLOCK] = lower
        near = band(cols_turned, level, BLOCK - RADIUS + shift_col, 3 * BLOCK)
        for y in range(blocks):
            for j in range(blocks):
                piece = jnp.zeros((BLOCK, BLOCK), BF16)
                if abs(j - y) <= 1:
                    piece = near[:, (j - y + 1) * BLOCK : (j - y + 2) * BLOCK]
                col_ref[s, y * BLOCK : (y + 1) * BLOCK, j * BLOCK : (j + 1) * BLOCK] = piece
    if blocks > 2:
        for outside, j in ((scen == 0, 0), (scen == lax.axis_size("scen") - 1, 2)):

            @pl.when(outside)
            def _():
                for s in range(scen_total):
                    col_ref[s, :, j * BLOCK : (j + 1) * BLOCK] = jnp.zeros((width, BLOCK), BF16)

    for s in range(scen_total):
        here = slice(s * BLOCK, (s + 1) * BLOCK)
        mine = col_ref[s, own_rows, :].T
        own_ref[:, here] = mine
        fold_ref[:, here] = dot(col_ref[s], mine).astype(BF16)


def lead_kernel(out):
    out[...] = jnp.zeros(out.shape, F32)


def pack_kernel(dwell, target, lead, out):
    tile = dwell.shape[0]
    odd = lax.rem(lax.axis_index("space"), 2)
    mine = pl.ds(pl.multiple_of(lax.axis_index("scen") * BLOCK, BLOCK), BLOCK)
    out[:BLOCK, :] = dwell[pl.ds(pl.multiple_of(odd * (tile - BLOCK), BLOCK), BLOCK), :]
    out[BLOCK:, :] = target[pl.ds(pl.multiple_of(odd * (tile - HALF), HALF), HALF), mine]


def clear_outside(blocks, ref):
    if blocks > 2:
        scen = lax.axis_index("scen")
        for outside, b in ((scen == 0, 0), (scen == lax.axis_size("scen") - 1, 2)):

            @pl.when(outside)
            def _():
                ref[:, b * BLOCK : (b + 1) * BLOCK] = jnp.zeros((ref.shape[0], BLOCK), BF16)


def terms_of(edge, dwell_rows, target_rows):
    rhs = []
    for s in range(dwell_rows.shape[1] // BLOCK):
        here = slice(s * BLOCK, (s + 1) * BLOCK)
        rhs += [dwell_rows[:, here], target_rows[:, here]]
    return dot(edge, jnp.concatenate(rhs, axis=0))


def send_kernel(blocks, scale, fold, own, edge, target, *refs):
    mids, (from_ref, to_inner, tile_ref, target_ends) = refs[:blocks], refs[blocks:]
    tile = tile_ref.shape[0]
    odd = lax.rem(lax.axis_index("space"), 2)
    for b, lane in enumerate(lanes_of(blocks)):
        tile_ref[:, lane] = mids[b][...]
    clear_outside(blocks, tile_ref)
    from_ref[...] = (dot(tile_ref[...], fold[...]) * scale[0:1, :]).astype(BF16)
    rows = pl.ds(pl.multiple_of((1 - odd) * (tile - HALF), HALF), HALF)
    target_ends[...] = jnp.zeros(target_ends.shape, BF16)
    target_ends[pl.ds(pl.multiple_of(odd * HALF, HALF), HALF), :] = target[rows, :]
    ends = (dot(target_ends[...], own[...]) * scale[1:2, :]).astype(BF16)
    rows = pl.ds(pl.multiple_of((1 - odd) * (tile - BLOCK), BLOCK), BLOCK)
    to_inner[...] = terms_of(edge[odd], from_ref[rows, :], ends).astype(BF16)


def own_kernel(scale, fwd, adj, own, from_dwell, target, dwell, partial_ref, target_all, rhs):
    scen_total, width = fwd.shape[0], own.shape[0]
    tile = target.shape[0]
    space = lax.axis_index("space")
    target_all[:HALF, :] = jnp.zeros((HALF, width), BF16)
    target_all[HALF : HALF + tile, :] = target[...]
    target_all[HALF + tile :, :] = jnp.zeros((HALF, width), BF16)
    from_target = (dot(target_all[...], own[...]) * scale[1:2, :]).astype(BF16)
    lane = lax.broadcasted_iota(jnp.int32, (BLOCK, 2 * BLOCK), 1)
    cuts = (
        (space == 0) & (lane < HALF),
        (space == lax.axis_size("space") - 1) & (lane >= 2 * BLOCK - HALF),
    )
    for b in range(2):
        lhs = []
        for s in range(scen_total):
            here = slice(s * BLOCK, (s + 1) * BLOCK)
            back = jnp.where(cuts[b], jnp.zeros((BLOCK, 2 * BLOCK), BF16), adj[s])
            upper, lower = dot(back[:, :BLOCK], fwd[s]), dot(back[:, BLOCK:], fwd[s])
            middle = (upper[:, BLOCK:] + lower[:, :BLOCK]).astype(BF16)
            if b == 0:
                lhs += [middle, lower[:, BLOCK:].astype(BF16), back]
            else:
                lhs += [upper[:, :BLOCK].astype(BF16), middle, back]
            at = 4 * s * BLOCK
            rhs[at : at + tile, :] = from_dwell[:, here]
            rhs[at + tile : at + tile + 2 * BLOCK, :] = from_target[b * BLOCK : (b + 2) * BLOCK, here]
        gradient = dot(jnp.concatenate(lhs, axis=1), rhs[...])
        half = slice(b * BLOCK, (b + 1) * BLOCK)
        partial_ref[half, :] = dwell[half, :].astype(F32) - STEP_SIZE * gradient


def finish_kernel(blocks, scale, fold, own, edge, partial, bound, inner, *refs):
    halos, refs = refs[blocks - 1 : blocks] + refs[: blocks - 1], refs[blocks:]
    out, dwell_halo, target_halo = refs
    tile, width = out.shape[0], own.shape[0]
    space = lax.axis_index("space")
    odd = lax.rem(space, 2)
    end = (space == 0) | (space == lax.axis_size("space") - 1)

    def step(at, gradient):
        half = pl.ds(pl.multiple_of(at * (tile - BLOCK), BLOCK), BLOCK)
        stepped = partial[half, :] - STEP_SIZE * gradient
        out[half, :] = jnp.where(
            bound[half, :] == 1, jnp.maximum(stepped, 0.0), stepped
        ).astype(BF16)

    @pl.when(end)
    def _():
        step(1 - odd, inner[...].astype(F32))
        step(odd, 0.0)

    @pl.when(jnp.logical_not(end))
    def _():
        goal_rows = pl.ds(pl.multiple_of(odd * HALF, HALF), HALF)
        target_halo[...] = jnp.zeros((BLOCK, width), BF16)
        for b, lane in enumerate(lanes_of(blocks)):
            dwell_halo[:, lane] = halos[b][:BLOCK, :]
            target_halo[goal_rows, lane] = halos[b][BLOCK:, :]
        clear_outside(blocks, dwell_halo)
        clear_outside(blocks, target_halo)
        from_dwell = (dot(dwell_halo[...], fold[...]) * scale[0:1, :]).astype(BF16)
        from_target = (dot(target_halo[...], own[...]) * scale[1:2, :]).astype(BF16)
        terms = terms_of(edge[odd], from_dwell, from_target)
        step(1 - odd, inner[...].astype(F32))
        step(odd, terms)


def shards(
    dwell_map, target_map, bound_mask, offsets, rate_index, rate_table, row_kernels, col_kernels
):
    tile = dwell_map.shape[0]
    n_space, n_scen = lax.axis_size("space"), lax.axis_size("scen")
    scen = lax.axis_index("scen")
    scen_total = offsets.shape[0]
    blocks = min(n_scen, 3)
    width = blocks * BLOCK
    sides = {1: [], 2: [1]}.get(n_scen, [-1, 1])

    def moved(x, partner):
        pairs = []
        for i in range(n_space):
            for j in range(n_scen):
                a, b = partner(i, j)
                pairs.append((a * n_scen + b % n_scen, i * n_scen + j))
        return lax.ppermute(x, ("space", "scen"), pairs)

    def side(cols):
        return lambda i, j: (i, j + cols)

    def inner(i, j):
        return i ^ 1, j

    def outer(cols):
        def partner(i, j):
            if i in (0, n_space - 1):
                return i, (j ^ 1 if n_scen % 2 == 0 else j)
            return ((i - 1) ^ 1) + 1, j + cols

        return partner

    def call(kernel, name, outs, scratch, flops, specs, *args, limit=32 * 1024 * 1024):
        return pl.pallas_call(
            kernel,
            out_shape=outs,
            in_specs=specs,
            out_specs=jax.tree.map(lambda _: VMEM, outs),
            scratch_shapes=scratch,
            compiler_params=pltpu.CompilerParams(vmem_limit_bytes=limit),
            cost_estimate=pl.CostEstimate(
                flops=flops, bytes_accessed=flops // 100, transcendentals=0
            ),
            name=name,
        )(*args)

    if n_scen <= 2:
        target = target_map
    else:
        target = lax.dynamic_slice_in_dim(
            jnp.pad(target_map, ((0, 0), (BLOCK, BLOCK))), scen * BLOCK, width, 1
        )
    neighbours = [moved(dwell_map, side(c)) for c in sides]
    wide = scen_total * BLOCK
    small = (
        offsets.T,
        rate_index.reshape(1, scen_total),
        rate_table.reshape(1, rate_table.shape[0]),
        row_kernels,
        col_kernels,
    )
    lead = call(lead_kernel, "lead", pltpu.VMEM((8, BLOCK), F32), [], 10**9, [])
    to_outer = call(
        pack_kernel,
        "pack",
        pltpu.VMEM((BLOCK + HALF, BLOCK), BF16),
        [],
        10**5,
        [VMEM] * 3,
        dwell_map,
        target_map,
        lead,
    )
    halos = [moved(to_outer, outer(c)) for c in [0] + sides]
    fwd, adj, fold, own, edge, scale = call(
        bands_kernel,
        "bands",
        (
            pltpu.VMEM((scen_total, BLOCK, 2 * BLOCK), BF16),
            pltpu.VMEM((scen_total, BLOCK, 2 * BLOCK), BF16),
            pltpu.VMEM((width, wide), BF16),
            pltpu.VMEM((width, wide), BF16),
            pltpu.VMEM((2, BLOCK, 2 * wide), BF16),
            pltpu.VMEM((8, wide), F32),
        ),
        [
            pltpu.VMEM((scen_total, width, width), BF16),
        ],
        10**8,
        [VMEM] * 5,
        *small,
    )
    from_dwell, to_inner = call(
        functools.partial(send_kernel, blocks),
        "send",
        (pltpu.VMEM((tile, wide), BF16), pltpu.VMEM((BLOCK, BLOCK), BF16)),
        [pltpu.VMEM((tile, width), BF16), pltpu.VMEM((BLOCK, width), BF16)],
        10**8,
        [VMEM] * (blocks + 5),
        scale,
        fold,
        own,
        edge,
        target,
        dwell_map,
        *neighbours,
    )
    inner_terms = moved(to_inner, inner)
    partial = call(
        own_kernel,
        "own",
        pltpu.VMEM((tile, BLOCK), F32),
        [
            pltpu.VMEM((tile + 2 * HALF, width), BF16),
            pltpu.VMEM((scen_total * (tile + 2 * BLOCK), BLOCK), BF16),
        ],
        10**9,
        [VMEM] * 7,
        scale,
        fwd,
        adj,
        own,
        from_dwell,
        target,
        dwell_map,
    )
    return call(
        functools.partial(finish_kernel, blocks),
        "finish",
        jax.ShapeDtypeStruct(dwell_map.shape, BF16),
        [pltpu.VMEM((BLOCK, width), BF16), pltpu.VMEM((BLOCK, width), BF16)],
        10**6,
        [VMEM] * (7 + blocks),
        scale,
        fold,
        own,
        edge,
        partial,
        bound_mask,
        inner_terms,
        *halos[1:],
        halos[0],
    )


def solution(mesh):
    return jax.shard_map(
        shards,
        mesh=mesh,
        in_specs=(
            P("space", "scen"),
            P("space", None),
            P("space", "scen"),
            P(),
            P(),
            P(),
            P(),
            P(),
        ),
        out_specs=P("space", "scen"),
        check_vma=False,
    )
```

```python
import functools

import jax
import jax.numpy as jnp
from jax import lax
from jax.experimental import pallas as pl
from jax.experimental.pallas import tpu as pltpu
from jax.sharding import PartitionSpec as P

KTAPS = 63
RADIUS = 31
BLOCK = 128
HALF = 64
STEP_SIZE = 1.0
BF16 = jnp.bfloat16
F32 = jnp.float32
VMEM = pl.BlockSpec(memory_space=pltpu.VMEM)
HBM = pl.BlockSpec(memory_space=pltpu.HBM)


def dot(a, b):
    return jnp.dot(a, b, preferred_element_type=F32)


def band(table, level, start, width):
    taps = table[0:1]
    for r in range(1, table.shape[0]):
        taps = jnp.where(level == r, table[r : r + 1], taps)
    line = jnp.concatenate([taps, jnp.zeros((1, width - KTAPS), F32)], axis=1)
    line = pltpu.roll(jnp.broadcast_to(line, (8, width)), start, 1)
    lines = jnp.broadcast_to(line[0:1], (BLOCK, width))
    return pltpu.roll(lines, 0, 1, stride=1, stride_axis=0).astype(BF16)


def number(one):
    return jnp.max(one.astype(F32)).astype(jnp.int32)


def lanes_of(blocks):
    if blocks == 2:
        own = lax.axis_index("scen") * BLOCK
        return [
            pl.ds(pl.multiple_of(own, BLOCK), BLOCK),
            pl.ds(pl.multiple_of(BLOCK - own, BLOCK), BLOCK),
        ]
    return [pl.ds((blocks - 1) // 2 * BLOCK, BLOCK), pl.ds(0, BLOCK), pl.ds(2 * BLOCK, BLOCK)][:blocks]


def bands_kernel(
    offsets, levels, rates, row_taps, col_taps,
    fwd_ref, adj_ref, fold_ref, own_ref, edge_ref, scale_ref, col_ref,
):
    scen_total, width = col_ref.shape[0], col_ref.shape[1]
    blocks = width // BLOCK
    scen = lax.axis_index("scen")
    own_rows = lanes_of(blocks)[0]
    turn = (
        lax.broadcasted_iota(jnp.int32, (KTAPS, KTAPS), 0)
        + lax.broadcasted_iota(jnp.int32, (KTAPS, KTAPS), 1)
        == KTAPS - 1
    )
    turn = turn.astype(F32).astype(BF16)
    rows, cols = row_taps[...], col_taps[...]
    rows_turned, cols_turned = dot(rows, turn), dot(cols, turn)
    rows = rows.astype(F32)

    for s in range(scen_total):
        level = levels[0:1, s : s + 1]
        rate = rates[0:1, 0:1]
        for r in range(1, rates.shape[1]):
            rate = jnp.where(level == r, rates[0:1, r : r + 1], rate)
        here = slice(s * BLOCK, (s + 1) * BLOCK)
        scale_ref[0:1, here] = jnp.broadcast_to(rate * rate * (1.0 / scen_total), (1, BLOCK))
        scale_ref[1:2, here] = jnp.broadcast_to(rate * (-1.0 / scen_total), (1, BLOCK))
        shift_row, shift_col = [number(offsets[k : k + 1, s : s + 1]) for k in range(2)]
        fwd = band(rows, level, HALF - RADIUS - shift_row, 2 * BLOCK)
        adj = band(rows_turned, level, HALF - RADIUS + shift_row, 2 * BLOCK)
        fwd_ref[s] = fwd
        adj_ref[s] = adj
        upper, lower = adj[:, :BLOCK], adj[:, BLOCK:]
        at = 2 * s * BLOCK
        edge_ref[0, :, at : at + BLOCK] = dot(upper, fwd[:, :BLOCK]).astype(BF16)
        edge_ref[0, :, at + BLOCK : at + 2 * BLOCK] = upper
        edge_ref[1, :, at : at + BLOCK] = dot(lower, fwd[:, BLOCK:]).astype(BF16)
        edge_ref[1, :, at + BLOCK : at + 2 * BLOCK] = lower
        near = band(cols_turned, level, BLOCK - RADIUS + shift_col, 3 * BLOCK)
        for y in range(blocks):
            for j in range(blocks):
                piece = jnp.zeros((BLOCK, BLOCK), BF16)
                if abs(j - y) <= 1:
                    piece = near[:, (j - y + 1) * BLOCK : (j - y + 2) * BLOCK]
                col_ref[s, y * BLOCK : (y + 1) * BLOCK, j * BLOCK : (j + 1) * BLOCK] = piece
    if blocks > 2:
        for outside, j in ((scen == 0, 0), (scen == lax.axis_size("scen") - 1, 2)):

            @pl.when(outside)
            def _():
                for s in range(scen_total):
                    col_ref[s, :, j * BLOCK : (j + 1) * BLOCK] = jnp.zeros((width, BLOCK), BF16)

    for s in range(scen_total):
        here = slice(s * BLOCK, (s + 1) * BLOCK)
        mine = col_ref[s, own_rows, :].T
        own_ref[:, here] = mine
        fold_ref[:, here] = dot(col_ref[s], mine).astype(BF16)


def lead_kernel(out):
    out[...] = jnp.zeros(out.shape, F32)


def pack_kernel(dwell, target, lead, out):
    tile = dwell.shape[0]
    odd = lax.rem(lax.axis_index("space"), 2)
    mine = pl.ds(pl.multiple_of(lax.axis_index("scen") * BLOCK, BLOCK), BLOCK)
    out[:BLOCK, :] = dwell[pl.ds(pl.multiple_of(odd * (tile - BLOCK), BLOCK), BLOCK), :]
    out[BLOCK:, :] = target[pl.ds(pl.multiple_of(odd * (tile - HALF), HALF), HALF), mine]


def clear_outside(blocks, ref):
    if blocks > 2:
        scen = lax.axis_index("scen")
        for outside, b in ((scen == 0, 0), (scen == lax.axis_size("scen") - 1, 2)):

            @pl.when(outside)
            def _():
                ref[:, b * BLOCK : (b + 1) * BLOCK] = jnp.zeros((ref.shape[0], BLOCK), BF16)


def terms_of(edge, dwell_rows, target_rows):
    rhs = []
    for s in range(dwell_rows.shape[1] // BLOCK):
        here = slice(s * BLOCK, (s + 1) * BLOCK)
        rhs += [dwell_rows[:, here], target_rows[:, here]]
    return dot(edge, jnp.concatenate(rhs, axis=0))


def send_kernel(blocks, scale, fold, own, edge, target, *refs):
    mids, (from_ref, to_inner, tile_ref, target_ends) = refs[:blocks], refs[blocks:]
    tile = tile_ref.shape[0]
    odd = lax.rem(lax.axis_index("space"), 2)
    for b, lane in enumerate(lanes_of(blocks)):
        tile_ref[:, lane] = mids[b][...]
    clear_outside(blocks, tile_ref)
    from_ref[...] = (dot(tile_ref[...], fold[...]) * scale[0:1, :]).astype(BF16)
    rows = pl.ds(pl.multiple_of((1 - odd) * (tile - HALF), HALF), HALF)
    target_ends[...] = jnp.zeros(target_ends.shape, BF16)
    target_ends[pl.ds(pl.multiple_of(odd * HALF, HALF), HALF), :] = target[rows, :]
    ends = (dot(target_ends[...], own[...]) * scale[1:2, :]).astype(BF16)
    rows = pl.ds(pl.multiple_of((1 - odd) * (tile - BLOCK), BLOCK), BLOCK)
    to_inner[...] = terms_of(edge[odd], from_ref[rows, :], ends).astype(BF16)


def own_kernel(scale, fwd, adj, own, from_dwell, target, dwell, partial_ref, target_all, rhs):
    scen_total, width = fwd.shape[0], own.shape[0]
    tile = target.shape[0]
    space = lax.axis_index("space")
    target_all[:HALF, :] = jnp.zeros((HALF, width), BF16)
    target_all[HALF : HALF + tile, :] = target[...]
    target_all[HALF + tile :, :] = jnp.zeros((HALF, width), BF16)
    from_target = (dot(target_all[...], own[...]) * scale[1:2, :]).astype(BF16)
    lane = lax.broadcasted_iota(jnp.int32, (BLOCK, 2 * BLOCK), 1)
    cuts = (
        (space == 0) & (lane < HALF),
        (space == lax.axis_size("space") - 1) & (lane >= 2 * BLOCK - HALF),
    )
    for b in range(2):
        lhs = []
        for s in range(scen_total):
            here = slice(s * BLOCK, (s + 1) * BLOCK)
            back = jnp.where(cuts[b], jnp.zeros((BLOCK, 2 * BLOCK), BF16), adj[s])
            upper, lower = dot(back[:, :BLOCK], fwd[s]), dot(back[:, BLOCK:], fwd[s])
            middle = (upper[:, BLOCK:] + lower[:, :BLOCK]).astype(BF16)
            if b == 0:
                lhs += [middle, lower[:, BLOCK:].astype(BF16), back]
            else:
                lhs += [upper[:, :BLOCK].astype(BF16), middle, back]
            at = 4 * s * BLOCK
            rhs[at : at + tile, :] = from_dwell[:, here]
            rhs[at + tile : at + tile + 2 * BLOCK, :] = from_target[b * BLOCK : (b + 2) * BLOCK, here]
        gradient = dot(jnp.concatenate(lhs, axis=1), rhs[...])
        half = slice(b * BLOCK, (b + 1) * BLOCK)
        partial_ref[half, :] = dwell[half, :].astype(F32) - STEP_SIZE * gradient


def finish_kernel(blocks, scale, fold, own, edge, partial, bound, inner, *refs):
    halos, refs = refs[blocks - 1 : blocks] + refs[: blocks - 1], refs[blocks:]
    out, dwell_halo, target_halo = refs
    tile, width = out.shape[0], own.shape[0]
    space = lax.axis_index("space")
    odd = lax.rem(space, 2)
    end = (space == 0) | (space == lax.axis_size("space") - 1)

    def step(at, gradient):
        half = pl.ds(pl.multiple_of(at * (tile - BLOCK), BLOCK), BLOCK)
        stepped = partial[half, :] - STEP_SIZE * gradient
        out[half, :] = jnp.where(
            bound[half, :] == 1, jnp.maximum(stepped, 0.0), stepped
        ).astype(BF16)

    @pl.when(end)
    def _():
        step(1 - odd, inner[...].astype(F32))
        step(odd, 0.0)

    @pl.when(jnp.logical_not(end))
    def _():
        goal_rows = pl.ds(pl.multiple_of(odd * HALF, HALF), HALF)
        target_halo[...] = jnp.zeros((BLOCK, width), BF16)
        for b, lane in enumerate(lanes_of(blocks)):
            dwell_halo[:, lane] = halos[b][:BLOCK, :]
            target_halo[goal_rows, lane] = halos[b][BLOCK:, :]
        clear_outside(blocks, dwell_halo)
        clear_outside(blocks, target_halo)
        from_dwell = (dot(dwell_halo[...], fold[...]) * scale[0:1, :]).astype(BF16)
        from_target = (dot(target_halo[...], own[...]) * scale[1:2, :]).astype(BF16)
        terms = terms_of(edge[odd], from_dwell, from_target)
        step(1 - odd, inner[...].astype(F32))
        step(odd, terms)


def shards(
    dwell_map, target_map, bound_mask, offsets, rate_index, rate_table, row_kernels, col_kernels
):
    tile = dwell_map.shape[0]
    n_space, n_scen = lax.axis_size("space"), lax.axis_size("scen")
    scen = lax.axis_index("scen")
    scen_total = offsets.shape[0]
    blocks = min(n_scen, 3)
    width = blocks * BLOCK
    sides = {1: [], 2: [1]}.get(n_scen, [-1, 1])

    def moved(x, partner):
        pairs = []
        for i in range(n_space):
            for j in range(n_scen):
                a, b = partner(i, j)
                pairs.append((a * n_scen + b % n_scen, i * n_scen + j))
        return lax.ppermute(x, ("space", "scen"), pairs)

    def side(cols):
        return lambda i, j: (i, j + cols)

    def inner(i, j):
        return i ^ 1, j

    def outer(cols):
        def partner(i, j):
            if i in (0, n_space - 1):
                return i, (j ^ 1 if n_scen % 2 == 0 else j)
            return ((i - 1) ^ 1) + 1, j + cols

        return partner

    def call(kernel, name, outs, scratch, flops, specs, *args, limit=32 * 1024 * 1024):
        return pl.pallas_call(
            kernel,
            out_shape=outs,
            in_specs=specs,
            out_specs=jax.tree.map(lambda _: VMEM, outs),
            scratch_shapes=scratch,
            compiler_params=pltpu.CompilerParams(vmem_limit_bytes=limit),
            cost_estimate=pl.CostEstimate(
                flops=flops, bytes_accessed=flops // 100, transcendentals=0
            ),
            name=name,
        )(*args)

    if n_scen <= 2:
        target = target_map
    else:
        target = lax.dynamic_slice_in_dim(
            jnp.pad(target_map, ((0, 0), (BLOCK, BLOCK))), scen * BLOCK, width, 1
        )
    neighbours = [moved(dwell_map, side(c)) for c in sides]
    wide = scen_total * BLOCK
    small = (
        offsets.T,
        rate_index.reshape(1, scen_total),
        rate_table.reshape(1, rate_table.shape[0]),
        row_kernels,
        col_kernels,
    )
    lead = call(lead_kernel, "lead", pltpu.VMEM((8, BLOCK), F32), [], 10**9, [])
    *small, lead = lax.optimization_barrier((*small, lead))
    to_outer = call(
        pack_kernel,
        "pack",
        pltpu.VMEM((BLOCK + HALF, BLOCK), BF16),
        [],
        10**5,
        [VMEM] * 3,
        dwell_map,
        target_map,
        lead,
    )
    halos = [moved(to_outer, outer(c)) for c in [0] + sides]
    fwd, adj, fold, own, edge, scale = call(
        bands_kernel,
        "bands",
        (
            pltpu.VMEM((scen_total, BLOCK, 2 * BLOCK), BF16),
            pltpu.VMEM((scen_total, BLOCK, 2 * BLOCK), BF16),
            pltpu.VMEM((width, wide), BF16),
            pltpu.VMEM((width, wide), BF16),
            pltpu.VMEM((2, BLOCK, 2 * wide), BF16),
            pltpu.VMEM((8, wide), F32),
        ),
        [
            pltpu.VMEM((scen_total, width, width), BF16),
        ],
        10**8,
        [VMEM] * 5,
        *small,
    )
    from_dwell, to_inner = call(
        functools.partial(send_kernel, blocks),
        "send",
        (pltpu.VMEM((tile, wide), BF16), pltpu.VMEM((BLOCK, BLOCK), BF16)),
        [pltpu.VMEM((tile, width), BF16), pltpu.VMEM((BLOCK, width), BF16)],
        10**8,
        [VMEM] * (blocks + 5),
        scale,
        fold,
        own,
        edge,
        target,
        dwell_map,
        *neighbours,
    )
    inner_terms = moved(to_inner, inner)
    partial = call(
        own_kernel,
        "own",
        pltpu.VMEM((tile, BLOCK), F32),
        [
            pltpu.VMEM((tile + 2 * HALF, width), BF16),
            pltpu.VMEM((scen_total * (tile + 2 * BLOCK), BLOCK), BF16),
        ],
        10**9,
        [VMEM] * 7,
        scale,
        fwd,
        adj,
        own,
        from_dwell,
        target,
        dwell_map,
    )
    return call(
        functools.partial(finish_kernel, blocks),
        "finish",
        jax.ShapeDtypeStruct(dwell_map.shape, BF16),
        [pltpu.VMEM((BLOCK, width), BF16), pltpu.VMEM((BLOCK, width), BF16)],
        10**6,
        [VMEM] * (7 + blocks),
        scale,
        fold,
        own,
        edge,
        partial,
        bound_mask,
        inner_terms,
        *halos[1:],
        halos[0],
    )


def solution(mesh):
    return jax.shard_map(
        shards,
        mesh=mesh,
        in_specs=(
            P("space", "scen"),
            P("space", None),
            P("space", "scen"),
            P(),
            P(),
            P(),
            P(),
            P(),
        ),
        out_specs=P("space", "scen"),
        check_vma=False,
    )
```

```python
import functools

import jax
import jax.numpy as jnp
from jax import lax
from jax.experimental import pallas as pl
from jax.experimental.pallas import tpu as pltpu
from jax.sharding import PartitionSpec as P

KTAPS = 63
RADIUS = 31
BLOCK = 128
HALF = 64
STEP_SIZE = 1.0
BF16 = jnp.bfloat16
F32 = jnp.float32
VMEM = pl.BlockSpec(memory_space=pltpu.VMEM)
HBM = pl.BlockSpec(memory_space=pltpu.HBM)


def dot(a, b):
    return jnp.dot(a, b, preferred_element_type=F32)


def band(table, level, start, width):
    taps = table[0:1]
    for r in range(1, table.shape[0]):
        taps = jnp.where(level == r, table[r : r + 1], taps)
    line = jnp.concatenate([taps, jnp.zeros((1, width - KTAPS), F32)], axis=1)
    line = pltpu.roll(jnp.broadcast_to(line, (8, width)), start, 1)
    lines = jnp.broadcast_to(line[0:1], (BLOCK, width))
    return pltpu.roll(lines, 0, 1, stride=1, stride_axis=0).astype(BF16)


def number(one):
    return jnp.max(one.astype(F32)).astype(jnp.int32)


def lanes_of(blocks):
    if blocks == 2:
        own = lax.axis_index("scen") * BLOCK
        return [
            pl.ds(pl.multiple_of(own, BLOCK), BLOCK),
            pl.ds(pl.multiple_of(BLOCK - own, BLOCK), BLOCK),
        ]
    return [pl.ds((blocks - 1) // 2 * BLOCK, BLOCK), pl.ds(0, BLOCK), pl.ds(2 * BLOCK, BLOCK)][:blocks]


def bands_kernel(
    offsets, levels, rates, row_taps, col_taps,
    fwd_ref, adj_ref, fold_ref, own_ref, edge_ref, scale_ref, col_ref,
):
    scen_total, width = col_ref.shape[0], col_ref.shape[1]
    blocks = width // BLOCK
    scen = lax.axis_index("scen")
    own_rows = lanes_of(blocks)[0]
    turn = (
        lax.broadcasted_iota(jnp.int32, (KTAPS, KTAPS), 0)
        + lax.broadcasted_iota(jnp.int32, (KTAPS, KTAPS), 1)
        == KTAPS - 1
    )
    turn = turn.astype(F32).astype(BF16)
    rows, cols = row_taps[...], col_taps[...]
    rows_turned, cols_turned = dot(rows, turn), dot(cols, turn)
    rows = rows.astype(F32)

    for s in range(scen_total):
        level = levels[0:1, s : s + 1]
        rate = rates[0:1, 0:1]
        for r in range(1, rates.shape[1]):
            rate = jnp.where(level == r, rates[0:1, r : r + 1], rate)
        here = slice(s * BLOCK, (s + 1) * BLOCK)
        scale_ref[0:1, here] = jnp.broadcast_to(rate * rate * (1.0 / scen_total), (1, BLOCK))
        scale_ref[1:2, here] = jnp.broadcast_to(rate * (-1.0 / scen_total), (1, BLOCK))
        shift_row, shift_col = [number(offsets[k : k + 1, s : s + 1]) for k in range(2)]
        fwd = band(rows, level, HALF - RADIUS - shift_row, 2 * BLOCK)
        adj = band(rows_turned, level, HALF - RADIUS + shift_row, 2 * BLOCK)
        fwd_ref[s] = fwd
        adj_ref[s] = adj
        upper, lower = adj[:, :BLOCK], adj[:, BLOCK:]
        at = 2 * s * BLOCK
        edge_ref[0, :, at : at + BLOCK] = dot(upper, fwd[:, :BLOCK]).astype(BF16)
        edge_ref[0, :, at + BLOCK : at + 2 * BLOCK] = upper
        edge_ref[1, :, at : at + BLOCK] = dot(lower, fwd[:, BLOCK:]).astype(BF16)
        edge_ref[1, :, at + BLOCK : at + 2 * BLOCK] = lower
        near = band(cols_turned, level, BLOCK - RADIUS + shift_col, 3 * BLOCK)
        for y in range(blocks):
            for j in range(blocks):
                piece = jnp.zeros((BLOCK, BLOCK), BF16)
                if abs(j - y) <= 1:
                    piece = near[:, (j - y + 1) * BLOCK : (j - y + 2) * BLOCK]
                col_ref[s, y * BLOCK : (y + 1) * BLOCK, j * BLOCK : (j + 1) * BLOCK] = piece
    if blocks > 2:
        for outside, j in ((scen == 0, 0), (scen == lax.axis_size("scen") - 1, 2)):

            @pl.when(outside)
            def _():
                for s in range(scen_total):
                    col_ref[s, :, j * BLOCK : (j + 1) * BLOCK] = jnp.zeros((width, BLOCK), BF16)

    for s in range(scen_total):
        here = slice(s * BLOCK, (s + 1) * BLOCK)
        mine = col_ref[s, own_rows, :].T
        own_ref[:, here] = mine
        fold_ref[:, here] = dot(col_ref[s], mine).astype(BF16)


def lead_kernel(out):
    out[...] = jnp.zeros(out.shape, F32)


def pack_kernel(dwell, target, lead, out):
    tile = dwell.shape[0]
    odd = lax.rem(lax.axis_index("space"), 2)
    mine = pl.ds(pl.multiple_of(lax.axis_index("scen") * BLOCK, BLOCK), BLOCK)
    out[:BLOCK, :] = dwell[pl.ds(pl.multiple_of(odd * (tile - BLOCK), BLOCK), BLOCK), :]
    out[BLOCK:, :] = target[pl.ds(pl.multiple_of(odd * (tile - HALF), HALF), HALF), mine]


def clear_outside(blocks, ref):
    if blocks > 2:
        scen = lax.axis_index("scen")
        for outside, b in ((scen == 0, 0), (scen == lax.axis_size("scen") - 1, 2)):

            @pl.when(outside)
            def _():
                ref[:, b * BLOCK : (b + 1) * BLOCK] = jnp.zeros((ref.shape[0], BLOCK), BF16)


def terms_of(edge, dwell_rows, target_rows):
    rhs = []
    for s in range(dwell_rows.shape[1] // BLOCK):
        here = slice(s * BLOCK, (s + 1) * BLOCK)
        rhs += [dwell_rows[:, here], target_rows[:, here]]
    return dot(edge, jnp.concatenate(rhs, axis=0))


def send_kernel(blocks, scale, fold, own, edge, target, *refs):
    mids, (from_ref, to_inner, tile_ref, target_ends) = refs[:blocks], refs[blocks:]
    tile = tile_ref.shape[0]
    odd = lax.rem(lax.axis_index("space"), 2)
    for b, lane in enumerate(lanes_of(blocks)):
        tile_ref[:, lane] = mids[b][...]
    clear_outside(blocks, tile_ref)
    from_ref[...] = (dot(tile_ref[...], fold[...]) * scale[0:1, :]).astype(BF16)
    rows = pl.ds(pl.multiple_of((1 - odd) * (tile - HALF), HALF), HALF)
    target_ends[...] = jnp.zeros(target_ends.shape, BF16)
    target_ends[pl.ds(pl.multiple_of(odd * HALF, HALF), HALF), :] = target[rows, :]
    ends = (dot(target_ends[...], own[...]) * scale[1:2, :]).astype(BF16)
    rows = pl.ds(pl.multiple_of((1 - odd) * (tile - BLOCK), BLOCK), BLOCK)
    to_inner[...] = terms_of(edge[odd], from_ref[rows, :], ends).astype(BF16)


def own_kernel(scale, fwd, adj, own, from_dwell, target, dwell, partial_ref, target_all, rhs):
    scen_total, width = fwd.shape[0], own.shape[0]
    tile = target.shape[0]
    space = lax.axis_index("space")
    target_all[:HALF, :] = jnp.zeros((HALF, width), BF16)
    target_all[HALF : HALF + tile, :] = target[...]
    target_all[HALF + tile :, :] = jnp.zeros((HALF, width), BF16)
    from_target = (dot(target_all[...], own[...]) * scale[1:2, :]).astype(BF16)
    lane = lax.broadcasted_iota(jnp.int32, (BLOCK, 2 * BLOCK), 1)
    cuts = (
        (space == 0) & (lane < HALF),
        (space == lax.axis_size("space") - 1) & (lane >= 2 * BLOCK - HALF),
    )
    for b in range(2):
        lhs = []
        for s in range(scen_total):
            here = slice(s * BLOCK, (s + 1) * BLOCK)
            back = jnp.where(cuts[b], jnp.zeros((BLOCK, 2 * BLOCK), BF16), adj[s])
            upper, lower = dot(back[:, :BLOCK], fwd[s]), dot(back[:, BLOCK:], fwd[s])
            middle = (upper[:, BLOCK:] + lower[:, :BLOCK]).astype(BF16)
            if b == 0:
                lhs += [middle, lower[:, BLOCK:].astype(BF16), back]
            else:
                lhs += [upper[:, :BLOCK].astype(BF16), middle, back]
            at = 4 * s * BLOCK
            rhs[at : at + tile, :] = from_dwell[:, here]
            rhs[at + tile : at + tile + 2 * BLOCK, :] = from_target[b * BLOCK : (b + 2) * BLOCK, here]
        gradient = dot(jnp.concatenate(lhs, axis=1), rhs[...])
        half = slice(b * BLOCK, (b + 1) * BLOCK)
        partial_ref[half, :] = dwell[half, :].astype(F32) - STEP_SIZE * gradient


def finish_kernel(blocks, scale, fold, own, edge, partial, bound, inner, *refs):
    halos, refs = refs[blocks - 1 : blocks] + refs[: blocks - 1], refs[blocks:]
    out, dwell_halo, target_halo = refs
    tile, width = out.shape[0], own.shape[0]
    space = lax.axis_index("space")
    odd = lax.rem(space, 2)
    end = (space == 0) | (space == lax.axis_size("space") - 1)

    def step(at, gradient):
        half = pl.ds(pl.multiple_of(at * (tile - BLOCK), BLOCK), BLOCK)
        stepped = partial[half, :] - STEP_SIZE * gradient
        out[half, :] = jnp.where(
            bound[half, :] == 1, jnp.maximum(stepped, 0.0), stepped
        ).astype(BF16)

    @pl.when(end)
    def _():
        step(1 - odd, inner[...].astype(F32))
        step(odd, 0.0)

    @pl.when(jnp.logical_not(end))
    def _():
        if blocks == 2:
            flip = lax.axis_index("scen") == 1

            def window(rows):
                mine, other = halos[0][rows, :], halos[1][rows, :]
                return jnp.where(
                    flip,
                    jnp.concatenate([other, mine], axis=1),
                    jnp.concatenate([mine, other], axis=1),
                )

            dwell_rows, target_rows = window(slice(0, BLOCK)), window(slice(BLOCK, BLOCK + HALF))
        else:
            for b, lane in enumerate(lanes_of(blocks)):
                dwell_halo[:, lane] = halos[b][:BLOCK, :]
                target_halo[:, lane] = halos[b][BLOCK:, :]
            clear_outside(blocks, dwell_halo)
            clear_outside(blocks, target_halo)
            dwell_rows, target_rows = dwell_halo[...], target_halo[...]
        from_dwell = (dot(dwell_rows, fold[...]) * scale[0:1, :]).astype(BF16)
        from_target = (dot(target_rows, own[...]) * scale[1:2, :]).astype(BF16)
        none = jnp.zeros_like(from_target)
        from_target = jnp.where(
            odd == 1,
            jnp.concatenate([none, from_target], axis=0),
            jnp.concatenate([from_target, none], axis=0),
        )
        terms = terms_of(edge[odd], from_dwell, from_target)
        step(1 - odd, inner[...].astype(F32))
        step(odd, terms)


def shards(
    dwell_map, target_map, bound_mask, offsets, rate_index, rate_table, row_kernels, col_kernels
):
    tile = dwell_map.shape[0]
    n_space, n_scen = lax.axis_size("space"), lax.axis_size("scen")
    scen = lax.axis_index("scen")
    scen_total = offsets.shape[0]
    blocks = min(n_scen, 3)
    width = blocks * BLOCK
    sides = {1: [], 2: [1]}.get(n_scen, [-1, 1])

    def moved(x, partner):
        pairs = []
        for i in range(n_space):
            for j in range(n_scen):
                a, b = partner(i, j)
                pairs.append((a * n_scen + b % n_scen, i * n_scen + j))
        return lax.ppermute(x, ("space", "scen"), pairs)

    def side(cols):
        return lambda i, j: (i, j + cols)

    def inner(i, j):
        return i ^ 1, j

    def outer(cols):
        def partner(i, j):
            if i in (0, n_space - 1):
                return i, (j ^ 1 if n_scen % 2 == 0 else j)
            return ((i - 1) ^ 1) + 1, j + cols

        return partner

    def call(kernel, name, outs, scratch, flops, specs, *args, limit=32 * 1024 * 1024):
        return pl.pallas_call(
            kernel,
            out_shape=outs,
            in_specs=specs,
            out_specs=jax.tree.map(lambda _: VMEM, outs),
            scratch_shapes=scratch,
            compiler_params=pltpu.CompilerParams(vmem_limit_bytes=limit),
            cost_estimate=pl.CostEstimate(
                flops=flops, bytes_accessed=flops // 100, transcendentals=0
            ),
            name=name,
        )(*args)

    if n_scen <= 2:
        target = target_map
    else:
        target = lax.dynamic_slice_in_dim(
            jnp.pad(target_map, ((0, 0), (BLOCK, BLOCK))), scen * BLOCK, width, 1
        )
    neighbours = [moved(dwell_map, side(c)) for c in sides]
    wide = scen_total * BLOCK
    small = (
        offsets.T,
        rate_index.reshape(1, scen_total),
        rate_table.reshape(1, rate_table.shape[0]),
        row_kernels,
        col_kernels,
    )
    lead = call(lead_kernel, "lead", pltpu.VMEM((8, BLOCK), F32), [], 10**9, [])
    *small, lead = lax.optimization_barrier((*small, lead))
    to_outer = call(
        pack_kernel,
        "pack",
        pltpu.VMEM((BLOCK + HALF, BLOCK), BF16),
        [],
        10**5,
        [VMEM] * 3,
        dwell_map,
        target_map,
        lead,
    )
    halos = [moved(to_outer, outer(c)) for c in [0] + sides]
    fwd, adj, fold, own, edge, scale = call(
        bands_kernel,
        "bands",
        (
            pltpu.VMEM((scen_total, BLOCK, 2 * BLOCK), BF16),
            pltpu.VMEM((scen_total, BLOCK, 2 * BLOCK), BF16),
            pltpu.VMEM((width, wide), BF16),
            pltpu.VMEM((width, wide), BF16),
            pltpu.VMEM((2, BLOCK, 2 * wide), BF16),
            pltpu.VMEM((8, wide), F32),
        ),
        [
            pltpu.VMEM((scen_total, width, width), BF16),
        ],
        10**8,
        [VMEM] * 5,
        *small,
    )
    from_dwell, to_inner = call(
        functools.partial(send_kernel, blocks),
        "send",
        (pltpu.VMEM((tile, wide), BF16), pltpu.VMEM((BLOCK, BLOCK), BF16)),
        [pltpu.VMEM((tile, width), BF16), pltpu.VMEM((BLOCK, width), BF16)],
        10**8,
        [VMEM] * (blocks + 5),
        scale,
        fold,
        own,
        edge,
        target,
        dwell_map,
        *neighbours,
    )
    inner_terms = moved(to_inner, inner)
    partial = call(
        own_kernel,
        "own",
        pltpu.VMEM((tile, BLOCK), F32),
        [
            pltpu.VMEM((tile + 2 * HALF, width), BF16),
            pltpu.VMEM((scen_total * (tile + 2 * BLOCK), BLOCK), BF16),
        ],
        10**9,
        [VMEM] * 7,
        scale,
        fwd,
        adj,
        own,
        from_dwell,
        target,
        dwell_map,
    )
    return call(
        functools.partial(finish_kernel, blocks),
        "finish",
        jax.ShapeDtypeStruct(dwell_map.shape, BF16),
        [pltpu.VMEM((BLOCK, width), BF16), pltpu.VMEM((HALF, width), BF16)],
        10**6,
        [VMEM] * (7 + blocks),
        scale,
        fold,
        own,
        edge,
        partial,
        bound_mask,
        inner_terms,
        *halos[1:],
        halos[0],
    )


def solution(mesh):
    return jax.shard_map(
        shards,
        mesh=mesh,
        in_specs=(
            P("space", "scen"),
            P("space", None),
            P("space", "scen"),
            P(),
            P(),
            P(),
            P(),
            P(),
        ),
        out_specs=P("space", "scen"),
        check_vma=False,
    )
```
